768 devices in a mesh: comp: 8 (over x, core), tile: 96 (over y, z).
Axes of the slice: x: 4, y: 8, z: 12, core: 2. Of those that a mesh axis runs over, the one named last changes fastest.
Arguments:
- initial: float32 [8, 12, 192, 384], P('comp', None, 'tile'), may hold values from -6 to 6
- cotangent: float32 [8, 12, 192, 384], P('comp', None, 'tile'), may hold values from -6 to 6
- spread_coef: float32 [8, 12, 192, 384], P('comp', None, 'tile'), may hold values from 0.4 to 1
- trajectory: float32 [4, 8, 12, 192, 384], P(None, 'comp', None, 'tile'), may hold values from 0.5 to 1.6
- mixing: float32 [8, 12, 12], P('comp')
- sea_mask: int32 [8, 192, 384], P('comp', 'tile'), may hold values 0 or 1
- src_group: int32 [8, 96, 96, 64], P('comp', 'tile'), may hold values from 0 to 7, as said below
- src_cell: int32 [8, 96, 96, 64], P('comp', 'tile'), may hold values from 0 to 767
- weight: float32 [8, 96, 96, 64], P('comp', 'tile'), may hold values from 0.25 to 1
- counts: int32 [8, 96, 96], P('comp', 'tile'), may hold values from 0 to 64, as said below
- dst_cell: int32 [8, 96, 96, 64], P('comp', 'tile'), may hold values from 0 to 767
Outputs:
- final_state: float32 [8, 12, 192, 384], P('comp', None, 'tile')
- gradient: float32 [8, 12, 192, 384], P('comp', None, 'tile')
The draws below stay inside these ranges and needn't reach their ends.
Inputs may be any that keep to these rules, and one draw needn't show every extreme that they name: `src_group`: the source group of a slot is an ocean group (index 6 or more) when the receiving group is an atmosphere group (index under 6), and an atmosphere group otherwise; it is the same for all slots of one pair of tiles. `counts`: in every group one receiving tile gets all 64 slots live from every sending tile.
All inputs are finite; a program needn't handle non-finite values. No bound on the sum of `sea_mask` on one device may be relied on, other than what follows from the above.
Results may differ from the reference program's by a relative error of at most 0.00015.
Values sent between devices are 32-bit elements; how exact they have to be, the bound alone decides.
A program may use at most 32 MiB of HBM per device.

```python
import math
import jax
import jax.numpy as jnp
from jax import lax

COLS = 384
LEV = 12
ROWS_DEV = 2
CAP = 64
INTERVALS = 2
SUBSTEPS = 2
GROUPS = 8
ATMOS = 6
TILES = 96
ROWS = 192
CELLS = 768
STEPS = 4


def draw_mixing(key, part):
    key = jax.random.fold_in(key, 11)
    shape = (GROUPS, LEV, LEV)
    noise = jax.random.normal(key, shape, jnp.float32)
    return 0.7 * jnp.eye(LEV, dtype=jnp.float32)[None] + 0.25 * LEV ** (-0.5) * noise


def draw_src_group(key, part):
    key = jax.random.fold_in(key, 12)
    pair_shape = (GROUPS, TILES, TILES, 1)
    owner = lax.broadcasted_iota(jnp.int32, pair_shape, 0)
    ocean_pick = ATMOS + jax.random.randint(key, pair_shape, 0, GROUPS - ATMOS)
    atmos_pick = jax.random.randint(jax.random.fold_in(key, 1), pair_shape, 0, ATMOS)
    chosen = jnp.where(owner < ATMOS, ocean_pick, atmos_pick)
    return jnp.broadcast_to(chosen, (GROUPS, TILES, TILES, CAP)).astype(jnp.int32)


def facing_cells(key, shape):
    own_tile = lax.broadcasted_iota(jnp.int32, shape, 1)
    other_tile = lax.broadcasted_iota(jnp.int32, shape, 2)
    half_rows = max(ROWS_DEV // 2, 1)
    any_row = jax.random.randint(key, shape, 0, ROWS_DEV)
    low_row = jax.random.randint(jax.random.fold_in(key, 1), shape, 0, half_rows)
    high_row = ROWS_DEV - 1 - jax.random.randint(jax.random.fold_in(key, 2), shape, 0, half_rows)
    row_pick = jnp.where(other_tile > own_tile, high_row, jnp.where(other_tile < own_tile, low_row, any_row))
    column_pick = jax.random.randint(jax.random.fold_in(key, 3), shape, 0, COLS)
    return (row_pick * COLS + column_pick).astype(jnp.int32)


def draw_src_cell(key, part):
    key = jax.random.fold_in(key, 14)
    return facing_cells(key, (GROUPS, TILES, TILES, CAP))


def draw_dst_cell(key, part):
    key = jax.random.fold_in(key, 15)
    return facing_cells(key, (GROUPS, TILES, TILES, CAP))


def draw_counts(key, part):
    key = jax.random.fold_in(key, 13)
    shape = (GROUPS, TILES, TILES)
    base_count = jax.random.randint(key, shape, 0, CAP + 1)
    hottest = jax.random.randint(jax.random.fold_in(key, 1), (GROUPS, 1, 1), 0, TILES)
    target = lax.broadcasted_iota(jnp.int32, shape, 2)
    return jnp.where(target == hottest, CAP, base_count).astype(jnp.int32)


def touch_ends(array, own_key, low, high):
    longest = array.shape.index(max(array.shape))
    spots = []
    for shift in (0, 1):
        where = [jax.random.randint(jax.random.fold_in(own_key, axis), (), 0, length) for axis, length in enumerate(array.shape)]
        where[longest] = (where[longest] + shift) % array.shape[longest]
        spots.append(tuple(where))
    return array.at[spots[0]].set(low).at[spots[1]].set(high)


def block_scale(stream_key, dims, split, smallest, largest):
    gain, own = 1.0, jax.random.fold_in(stream_key, 6)
    for position, parts in split:
        steps = jnp.exp(jax.random.uniform(jax.random.fold_in(own, position), (parts,), jnp.float32, smallest / len(split), largest / len(split)))
        gain = gain * jnp.repeat(steps, dims[position] // parts).reshape([-1 if axis == position else 1 for axis in range(len(dims))])
    return gain


def normal_values(own_key, shape, spread, limit, shards=(), held_as=jnp.bfloat16):
    result = jax.random.normal(own_key, shape, jnp.float32) * spread
    if len(shards) > 0:
        result = block_scale(own_key, shape, shards, -0.22, 0.18) * result
    return jnp.clip(result, min=-limit, max=limit).astype(held_as)


def setup_inputs(seed: int = 0) -> dict:
    splits = jax.random.split(jax.random.key(seed), 12)
    return {
        "initial": normal_values(splits[0], (GROUPS, LEV, ROWS, COLS), 1.0, 6.0, ((0, 8), (2, 96)), jnp.float32),
        "cotangent": normal_values(splits[1], (GROUPS, LEV, ROWS, COLS), 1.0, 6.0, ((0, 8), (2, 96)), jnp.float32),
        "spread_coef": jnp.clip(jnp.exp(math.log(1.0) - 0.9162907 * jax.random.uniform(splits[2], (GROUPS, LEV, ROWS, COLS), jnp.float32) ** block_scale(splits[2], (GROUPS, LEV, ROWS, COLS), ((0, 8), (2, 96)), -0.2, 0.2)), 0.4, 1.0),
        "trajectory": jnp.clip(jnp.exp(math.log(1.6) - 1.1631508 * jax.random.uniform(splits[3], (STEPS, GROUPS, LEV, ROWS, COLS), jnp.float32) ** block_scale(splits[3], (STEPS, GROUPS, LEV, ROWS, COLS), ((1, 8), (3, 96)), -0.2, 0.2)), 0.5, 1.6),
        "mixing": draw_mixing(jax.random.fold_in(splits[11], 71), 0),
        "sea_mask": touch_ends((jax.random.randint(splits[5], (GROUPS, ROWS, COLS), 0, 10) < 7).astype(jnp.int32), jax.random.fold_in(splits[5], 1), 0, 1),
        "src_group": draw_src_group(jax.random.fold_in(splits[11], 71), 0),
        "src_cell": draw_src_cell(jax.random.fold_in(splits[11], 71), 0),
        "weight": jnp.clip(0.25 + 0.75 * jax.random.uniform(splits[8], (GROUPS, TILES, TILES, CAP), jnp.float32) ** block_scale(splits[8], (GROUPS, TILES, TILES, CAP), ((0, 8), (1, 96)), -0.2, 0.2), 0.25, 1.0),
        "counts": draw_counts(jax.random.fold_in(splits[11], 71), 0),
        "dst_cell": draw_dst_cell(jax.random.fold_in(splits[11], 71), 0),
    }


SPREAD = 0.12

def laplace(field_state):
    padded = jnp.pad(field_state, ((0, 0), (0, 0), (1, 1), (1, 1)))
    total = padded[:, :, 2:, 1:-1] + padded[:, :, :-2, 1:-1]
    total = total + padded[:, :, 1:-1, 2:] + padded[:, :, 1:-1, :-2]
    return total - 4.0 * field_state

def advance(field_state, spread_coef, mixing, factor):
    diffused = field_state + SPREAD * spread_coef * laplace(spread_coef * field_state)
    mixed_state = jnp.einsum('glm,gmrc->glrc', mixing, diffused, precision=lax.Precision.HIGHEST)
    return factor * mixed_state

def couple(field_state, sea_mask, src_group, src_cell, weight, counts, dst_cell):
    surface = field_state[:, 0].reshape(GROUPS, TILES, CELLS)
    tile_ids = jnp.arange(TILES, dtype=jnp.int32)[None, :, None, None]
    live_mask = jnp.arange(CAP, dtype=jnp.int32)[None, None, None, :] < counts[..., None]
    values = weight * live_mask.astype(jnp.float32) * surface[src_group, tile_ids, src_cell]
    values = jnp.swapaxes(values, 1, 2)
    group_ids = jnp.arange(GROUPS, dtype=jnp.int32)[:, None, None, None]
    dest_ids = jnp.arange(TILES, dtype=jnp.int32)[None, :, None, None]
    flat_index = (group_ids * TILES + dest_ids) * CELLS + dst_cell
    forcing = jax.ops.segment_sum(values.reshape(-1), flat_index.reshape(-1), num_segments=GROUPS * TILES * CELLS)
    forcing = forcing.reshape(GROUPS, ROWS, COLS) * sea_mask.astype(jnp.float32)
    return field_state.at[:, 0].add(forcing)

def reference(initial, cotangent, spread_coef, trajectory, mixing, sea_mask, src_group, src_cell, weight, counts, dst_cell):

    def linear_map(start_state):
        field_state = start_state
        for interval in range(INTERVALS):
            field_state = couple(field_state, sea_mask, src_group, src_cell, weight, counts, dst_cell)
            for substep in range(SUBSTEPS):
                field_state = advance(field_state, spread_coef, mixing, trajectory[interval * SUBSTEPS + substep])
        return field_state
    final_state, pullback = jax.vjp(linear_map, initial)
    gradient, = pullback(cotangent)
    return (final_state, gradient)
```

```python
import functools

import jax
import jax.numpy as jnp
from jax import lax
from jax.experimental import pallas as pl
from jax.experimental.pallas import tpu as pltpu
from jax.sharding import PartitionSpec as P

MESH = pl.DeviceIdType.MESH
SPREAD = 0.12
NG, NT, LEV, COLS, CAP = 8, 96, 12, 384, 64
HI = 6
F32, BF16, I32 = jnp.float32, jnp.bfloat16, jnp.int32

S0, SP, U1, T2, F1, T0, A1, U2, FF1, TB1, F2, Q1, S1, A2, FF2, TB2 = range(16)


def kernel(
    init_ref, cot_ref, spread_ref, traj_ref, mix_ref, sea_ref, srcg_ref, srcc_ref, w_ref, cnt_ref, dst_ref,
    outf_ref, outg_ref,
    sp, u1, t2, f1, t0, u2, f2, ff1, ff2, q1, ev1, ev2, ts1, ts2, tr1, tr2, snd1, snd2, rcv1, rcv2,
    wa, xa, ya, wb, own1, own3, adj, mb, mtb, seat, mtab, gi, slo, shi, wv, rlo, rrow, rw, val, onehot,
    ssem, rsem,
):
    g = lax.axis_index("comp")
    t = lax.axis_index("tile")
    right, left = lax.rem(t + 1, NT), lax.rem(t + NT - 1, NT)

    barrier = pltpu.get_barrier_semaphore()

    @pl.loop(1, NT)
    def _(j):
        pl.semaphore_signal(barrier, inc=1, device_id=(g, lax.rem(t + j, NT)), device_id_type=MESH)

    @pl.loop(1, NG)
    def _(j):
        pl.semaphore_signal(barrier, inc=1, device_id=(lax.rem(g + j, NG), t), device_id_type=MESH)

    def remote(k, src, dst, dev):
        return pltpu.make_async_remote_copy(
            src_ref=src, dst_ref=dst, send_sem=ssem.at[k], recv_sem=rsem.at[k], device_id=dev, device_id_type=MESH
        )

    def halo_send(k, buf):
        remote(k, buf.at[2:4], buf.at[0:2], (g, right)).start()
        remote(k, buf.at[2:4], buf.at[4:6], (g, left)).start()

    def wait_bytes(sem, k, ref):
        pltpu.make_async_copy(ref, ref, sem.at[k]).wait()

    def halo_recv(k, buf):
        wait_bytes(rsem, k, buf.at[0:4])

    def halo_sent(k, buf):
        wait_bytes(ssem, k, buf.at[0:4])

    def gather_send(k, ev):
        @pl.loop(1, NG)
        def _(j):
            remote(k, ev.at[g], ev.at[g], (lax.rem(g + j, NG), t)).start()

    def sum_send(k, ts, tr):
        @pl.loop(1, NG)
        def _(j):
            d = lax.rem(g + j, NG)
            remote(k, ts.at[d], tr.at[g], (d, t)).start()
        tr[g] = ts[g]

    def slots_send(k, snd, rcv):
        @pl.loop(1, NT)
        def _(j):
            d = lax.rem(t + j, NT)
            remote(k, snd.at[d], rcv.at[t], (g, d)).start()
        rcv[t] = snd[t]

    def strip(ref, r):
        return ref[:, r, :]

    lane = lax.broadcasted_iota(I32, (LEV, COLS), 1)

    def laplace(w, r):
        mid = w[r]
        west = jnp.where(lane == 0, 0.0, pltpu.roll(mid, 1, 1))
        east = jnp.where(lane == COLS - 1, 0.0, pltpu.roll(mid, COLS - 1, 1))
        return w[r + 1] + w[r - 1] + east + west - 4.0 * mid

    def mix_row(x, r, cols):
        parts = []
        for c in range(3):
            ls = slice(c * 128, (c + 1) * 128)
            acc = cols[0] * x[r, 0:1, ls]
            for m in range(1, LEV):
                acc = acc + cols[m] * x[r, m : m + 1, ls]
            parts.append(acc)
        return jnp.concatenate(parts, axis=1)

    def forward_pair(f, ta, tb_row, put):
        @pl.loop(0, 6)
        def _(r):
            wa[r] = sp[r] * f[r]

        @pl.loop(1, 5)
        def _(r):
            xa[r] = f[r] + SPREAD * sp[r] * laplace(wa, r)

        @pl.loop(1, 5)
        def _(r):
            y = ta[r] * mix_row(xa, r, mb)
            ya[r] = y
            wb[r] = sp[r] * y

        @pl.loop(2, 4)
        def _(r):
            xa[r] = ya[r] + SPREAD * sp[r] * laplace(wb, r)

        for r in (2, 3):
            put(r, tb_row(r) * mix_row(xa, r, mb))

    def adjoint_pair(u, ta):
        @pl.loop(0, 6)
        def _(r):
            wa[r] = sp[r] * u[r]

        @pl.loop(1, 5)
        def _(r):
            xa[r] = ta[r] * (u[r] + SPREAD * sp[r] * laplace(wa, r))

        @pl.loop(1, 5)
        def _(r):
            y = mix_row(xa, r, mtb)
            ya[r] = y
            wb[r] = sp[r] * y

        @pl.loop(2, 4)
        def _(r):
            adj[r] = ya[r] + SPREAD * sp[r] * laplace(wb, r)

    def surface_rows(get):
        return [get(r)[:, c * 128 : (c + 1) * 128] for r in (2, 3) for c in range(3)]

    def put_surface(ev, get):
        for h, row in enumerate(surface_rows(get)):
            ev[g, h : h + 1, :] = row

    def put_masked():
        for h, row in enumerate(surface_rows(lambda r: adj[r, 0:1, :])):
            mtab[h : h + 1, :] = row * seat[h : h + 1, :]

    half = lax.broadcasted_iota(I32, (8, 128), 1) < CAP

    def gather_adjoint():
        @pl.loop(0, NT // 8)
        def _(i):
            rows = pl.ds(pl.multiple_of(i * 8, 8), 8)
            lo, hi = slo[rows, :], shi[rows, :]
            out = jnp.zeros((8, 128), F32)
            for h in range(HI):
                table = jnp.broadcast_to(mtab[h : h + 1, :], (8, 128))
                out = jnp.where(hi == h, jnp.take_along_axis(table, lo, axis=1, mode="promise_in_bounds"), out)
            val[rows, :] = out

    def gather_forward(ev, snd):
        @pl.loop(0, NT // 8)
        def _(i):
            rows = pl.ds(pl.multiple_of(i * 8, 8), 8)
            lo, hi, owner = slo[rows, :], shi[rows, :], gi[rows, :]
            out = jnp.zeros((8, 128), F32)
            for h in range(HI):
                table = jnp.broadcast_to(ev[0, h : h + 1, :], (8, 128))
                for s in range(1, NG):
                    table = jnp.where(owner == s, ev[s, h : h + 1, :], table)
                out = jnp.where(hi == h, jnp.take_along_axis(table, lo, axis=1, mode="promise_in_bounds"), out)
            out = jnp.where(half, out, val[rows, :]) * wv[rows, :]
            snd.reshape(NT, 128)[rows, :] = out

    row_id = lax.broadcasted_iota(I32, (56, 128), 0)

    def scatter(rcv):
        def body(i, acc):
            rows = pl.ds(pl.multiple_of(i * 8, 8), 8)
            v = rcv.reshape(NT, 128)[rows, :] * rw[rows, :]
            where = rrow[rows, :]
            top = v.astype(BF16).astype(F32)
            rest = v - top
            mid = rest.astype(BF16).astype(F32)
            low = rest - mid
            blocks = []
            for j in range(8):
                hit = row_id == where[j : j + 1, :]
                blocks.append(
                    jnp.concatenate([jnp.where(hit, p[j : j + 1, :], 0.0) for p in (top, mid, low)], axis=0).astype(BF16)
                )
            m = jnp.concatenate(blocks, axis=1)
            return acc + lax.dot_general(m, onehot[i], (((1,), (1,)), ((), ())), preferred_element_type=F32)

        acc = lax.fori_loop(0, NT // 8, body, jnp.zeros((168, 128), F32))
        return acc[0:56] + acc[56:112] + acc[112:168]

    def put_forcing(total, ff):
        for h in range(HI):
            ff[2 + h // 3, 0:1, (h % 3) * 128 : (h % 3 + 1) * 128] = total[h : h + 1, :] * seat[h : h + 1, :]

    def put_terms(total, ts):
        for s in range(NG):
            ts[s, 0:HI, :] = total[8 + s * HI : 8 + (s + 1) * HI, :]

    def term_sum(tr):
        total = tr[0]
        for s in range(1, NG):
            total = total + tr[s]
        return total

    for m in range(LEV):
        mb[m] = jnp.broadcast_to(mix_ref[:, m : m + 1], (LEV, 128))
        diag = lax.broadcasted_iota(I32, (LEV, LEV), 0) == lax.broadcasted_iota(I32, (LEV, LEV), 1)
        column = jnp.sum(jnp.where(diag, mix_ref[m : m + 1, :], 0.0), axis=1, keepdims=True)
        mtb[m] = jnp.broadcast_to(column, (LEV, 128))
    for r in (0, 1):
        f1[2 + r] = strip(init_ref, r)
        sp[2 + r] = strip(spread_ref, r)
        t0[2 + r] = strip(traj_ref.at[0], r)
        t2[2 + r] = strip(traj_ref.at[2], r)
        own1[2 + r] = strip(traj_ref.at[1], r)
        own3[2 + r] = strip(traj_ref.at[3], r)
        xa[2 + r] = own3[2 + r] * strip(cot_ref, r)
    for r in (2, 3):
        u1[r] = mix_row(xa, r, mtb)
    put_surface(ev1, lambda r: f1[r, 0:1, :])

    pl.semaphore_wait(barrier, NT + NG - 2)
    gather_send(S0, ev1)
    halo_send(SP, sp)
    halo_send(U1, u1)
    halo_send(T2, t2)
    halo_send(F1, f1)
    halo_send(T0, t0)

    for h in range(HI):
        seat[h : h + 1, :] = sea_ref[h // 3 : h // 3 + 1, (h % 3) * 128 : (h % 3 + 1) * 128].astype(F32)
    diag = lax.broadcasted_iota(I32, (NT, NT), 0) == lax.broadcasted_iota(I32, (NT, NT), 1)
    live = jnp.sum(jnp.where(diag, cnt_ref[...].astype(F32), 0.0), axis=1, keepdims=True)
    slot = lax.broadcasted_iota(I32, (NT, CAP), 1).astype(F32)
    weight = w_ref[...] * jnp.where(slot < live, 1.0, 0.0)
    ones = jnp.ones((NT, CAP), F32)
    wv[...] = jnp.concatenate([weight, ones], axis=1)
    rw[...] = jnp.concatenate([ones, weight], axis=1)
    srcc, dstc, srcg = srcc_ref[...], dst_ref[...], srcg_ref[...]
    gi[...] = jnp.concatenate([srcg, srcg], axis=1)
    send_cell = jnp.concatenate([srcc, dstc], axis=1)
    slo[...] = jnp.bitwise_and(send_cell, 127)
    shi[...] = jnp.right_shift(send_cell, 7)
    rlo[...] = jnp.concatenate([jnp.bitwise_and(dstc, 127), jnp.bitwise_and(srcc, 127)], axis=1)
    rrow[...] = jnp.concatenate([jnp.right_shift(dstc, 7), 8 + HI * srcg + jnp.right_shift(srcc, 7)], axis=1)

    halo_recv(SP, sp)
    halo_recv(U1, u1)
    halo_recv(T2, t2)
    sp[0:2] = jnp.where(t > 0, sp[0:2], 0.0)
    sp[4:6] = jnp.where(t < NT - 1, sp[4:6], 0.0)
    adjoint_pair(u1, t2)
    put_masked()
    gather_adjoint()
    wait_bytes(rsem, S0, ev1.at[0 : NG - 1])
    gather_forward(ev1, snd1)
    slots_send(A1, snd1, rcv1)

    for r in (2, 3):
        xa[r] = own1[r] * adj[r]
    for r in (2, 3):
        u2[r] = mix_row(xa, r, mtb)
    halo_send(U2, u2)

    cell = lax.broadcasted_iota(I32, (128, 128), 0)

    @pl.loop(0, NT // 8)
    def _(i):
        rows = rlo[pl.ds(pl.multiple_of(i * 8, 8), 8), :]
        for j in range(8):
            hit = jnp.where(cell == rows[j : j + 1, :], 1.0, 0.0).astype(BF16)
            onehot[i, :, j * 128 : (j + 1) * 128] = hit

    halo_recv(F1, f1)
    halo_recv(T0, t0)
    halo_sent(F1, f1)
    wait_bytes(rsem, A1, rcv1.at[0 : NT - 1])
    total = scatter(rcv1)
    put_forcing(total, ff1)
    halo_send(FF1, ff1)
    put_terms(total, ts1)
    sum_send(TB1, ts1, tr1)
    halo_recv(FF1, ff1)
    for r in range(6):
        f1[r, 0:1, :] = f1[r, 0:1, :] + ff1[r]

    def put_f2(r, value):
        f2[r] = value

    forward_pair(f1, t0, lambda r: own1[r], put_f2)
    put_surface(ev2, lambda r: f2[r, 0:1, :])
    gather_send(S1, ev2)
    halo_send(F2, f2)

    wait_bytes(rsem, TB1, tr1.at[0 : NG - 1])
    part = term_sum(tr1)
    for h in range(HI):
        ls = slice((h % 3) * 128, (h % 3 + 1) * 128)
        q1[2 + h // 3, 0:1, ls] = part[h : h + 1, :] * own1[2 + h // 3, 0:1, ls]
    halo_send(Q1, q1)
    halo_recv(U2, u2)
    halo_sent(U2, u2)
    halo_recv(Q1, q1)
    for r in range(6):
        u2[r] = u2[r] + jnp.concatenate([mtb[0]] * 3, axis=1) * q1[r]
    adjoint_pair(u2, t0)
    put_masked()
    gather_adjoint()
    wait_bytes(rsem, S1, ev2.at[0 : NG - 1])
    gather_forward(ev2, snd2)
    slots_send(A2, snd2, rcv2)
    halo_recv(F2, f2)
    halo_sent(F2, f2)

    wait_bytes(ssem, S0, ev1.at[0 : NG - 1])
    wait_bytes(ssem, S1, ev2.at[0 : NG - 1])
    wait_bytes(ssem, TB1, tr1.at[0 : NG - 1])
    wait_bytes(ssem, A1, rcv1.at[0 : NT - 1])
    for k, buf in ((SP, sp), (U1, u1), (T2, t2), (T0, t0), (FF1, ff1), (Q1, q1)):
        halo_sent(k, buf)

    wait_bytes(rsem, A2, rcv2.at[0 : NT - 1])
    total = scatter(rcv2)
    put_forcing(total, ff2)
    halo_send(FF2, ff2)
    put_terms(total, ts2)
    sum_send(TB2, ts2, tr2)
    halo_recv(FF2, ff2)
    for r in range(6):
        f2[r, 0:1, :] = f2[r, 0:1, :] + ff2[r]

    def put_out(r, value):
        outf_ref[:, r - 2, :] = value

    forward_pair(f2, t2, lambda r: own3[r], put_out)
    wait_bytes(rsem, TB2, tr2.at[0 : NG - 1])
    part = term_sum(tr2)
    for h in range(HI):
        ls = slice((h % 3) * 128, (h % 3 + 1) * 128)
        adj[2 + h // 3, 0:1, ls] = adj[2 + h // 3, 0:1, ls] + part[h : h + 1, :]
    for r in (2, 3):
        outg_ref[:, r - 2, :] = adj[r]
    wait_bytes(ssem, A2, rcv2.at[0 : NT - 1])
    halo_sent(FF2, ff2)
    wait_bytes(ssem, TB2, tr2.at[0 : NG - 1])


def per_device(
    initial, cotangent, spread_coef, trajectory, mixing, sea_mask, src_group, src_cell, weight, counts, dst_cell
):
    field = lambda rows: pltpu.VMEM((rows, LEV, COLS), F32)
    line = pltpu.VMEM((6, 1, COLS), F32)
    eight = pltpu.VMEM((NG, 8, 128), F32)
    slots = pltpu.VMEM((NT, 1, 128), F32)
    columns = pltpu.VMEM((LEV, LEV, 128), F32)
    table = pltpu.VMEM((8, 128), F32)
    ints = pltpu.VMEM((NT, 128), I32)
    floats = pltpu.VMEM((NT, 128), F32)
    final, gradient = pl.pallas_call(
        kernel,
        out_shape=[jax.ShapeDtypeStruct((LEV, 2, COLS), F32)] * 2,
        in_specs=[pl.BlockSpec(memory_space=pltpu.VMEM)] * 11,
        out_specs=[pl.BlockSpec(memory_space=pltpu.VMEM)] * 2,
        scratch_shapes=[field(6)] * 7
        + [line] * 3
        + [eight] * 6
        + [slots] * 4
        + [field(6)] * 7
        + [columns] * 2
        + [table] * 2
        + [ints, ints, ints, floats, ints, ints, floats, floats]
        + [pltpu.VMEM((NT // 8, 128, 1024), BF16)]
        + [pltpu.SemaphoreType.DMA((16,))] * 2,
        compiler_params=pltpu.CompilerParams(
            collective_id=0, has_side_effects=True, vmem_limit_bytes=40 * 1024 * 1024
        ),
    )(
        initial[0], cotangent[0], spread_coef[0], trajectory[:, 0], mixing[0], sea_mask[0],
        src_group[0, 0], src_cell[0, 0], weight[0, 0], counts[0], dst_cell[0, 0],
    )
    return final[None], gradient[None]


def solution(mesh):
    return jax.shard_map(
        per_device,
        mesh=mesh,
        in_specs=(
            P("comp", None, "tile", None),
            P("comp", None, "tile", None),
            P("comp", None, "tile", None),
            P(None, "comp", None, "tile", None),
            P("comp", None, None),
            P("comp", "tile", None),
            P("comp", "tile", None, None),
            P("comp", "tile", None, None),
            P("comp", "tile", None, None),
            P("comp", "tile", None),
            P("comp", "tile", None, None),
        ),
        out_specs=(P("comp", None, "tile", None), P("comp", None, "tile", None)),
        check_vma=False,
    )
```

```python
import functools

import jax
import jax.numpy as jnp
from jax import lax
from jax.experimental import pallas as pl
from jax.experimental.pallas import tpu as pltpu
from jax.sharding import PartitionSpec as P

MESH = pl.DeviceIdType.MESH
SPREAD = 0.12
NG, NATM, NT, LEV, COLS, CAP = 8, 6, 96, 12, 384, 64
NY, NZ = 8, 12
HI = 6
BLOCKS = NT // 8
F32, BF16, I32 = jnp.float32, jnp.bfloat16, jnp.int32

S0, SP, U1, T2, F1, T0, A1, U2, TB1, F2, S1, A2, TB2, ST, DN = range(15)


def tile_offsets():
    offsets = [(a, b) for a in range(NY) for b in range(NZ) if (a, b) != (0, 0)]
    return sorted(offsets, key=lambda o: -(min(o[0], NY - o[0]) + min(o[1], NZ - o[1])))


def kernel(
    init_ref, cot_ref, spread_ref, traj_ref, mix_ref, sea_ref, srcg_ref, srcc_ref, w_ref, cnt_ref, dst_ref,
    outf_ref, outg_ref,
    sp, u1, t2, f1, t0, u2, f2, wa, xa, ya, wb, own1, own3, adj,
    st, dn, ev1, ev2, ts1, ts2, tr1, tr2, snd1, snd2, rcv1, rcv2,
    mb, mtb, seat, mtab, gi, slo, shi, rlo, rrow, rloh, rrowh, wv, rw, val, onehot, onehot_h,
    ssem, rsem,
):
    g = lax.axis_index("comp")
    t = lax.axis_index("tile")
    y, z = t // NZ, lax.rem(t, NZ)
    right, left = lax.rem(t + 1, NT), lax.rem(t + NT - 1, NT)
    atmos = g < NATM
    ocean = g >= NATM
    me = jnp.where(atmos, g, g - NATM)
    sides = (left, t, right)
    ys = [lax.rem(y + a, NY) * NZ for a in range(NY)]
    zs = [lax.rem(z + b, NZ) for b in range(NZ)]
    tiles = [ys[a] + zs[b] for a, b in tile_offsets()]

    def each_partner(act):
        @pl.when(atmos)
        def _():
            for p in range(NG - NATM):
                act(p, NATM + p)

        @pl.when(ocean)
        def _():
            for p in range(NATM):
                act(p, p)

    barrier = pltpu.get_barrier_semaphore()

    def greet(dev):
        pl.semaphore_signal(barrier, inc=1, device_id=dev, device_id_type=MESH)

    each_partner(lambda p, d: [greet((d, s)) for s in (t, left, right)])
    for dev in tiles:
        greet((g, dev))

    def remote(k, src, dst, dev):
        return pltpu.make_async_remote_copy(
            src_ref=src, dst_ref=dst, send_sem=ssem.at[k], recv_sem=rsem.at[k], device_id=dev, device_id_type=MESH
        )

    def halo_send(k, buf):
        remote(k, buf.at[2:4], buf.at[0:2], (g, right)).start()
        remote(k, buf.at[2:4], buf.at[4:6], (g, left)).start()

    def rim_send(k, buf):
        remote(k, buf.at[3:4], buf.at[1:2], (g, right)).start()
        remote(k, buf.at[2:3], buf.at[4:5], (g, left)).start()

    def wait_bytes(sem, k, ref):
        pltpu.make_async_copy(ref, ref, sem.at[k]).wait()

    def partner_wait(sem, k, buf):
        @pl.when(atmos)
        def _():
            wait_bytes(sem, k, buf.at[0 : NG - NATM])

        @pl.when(ocean)
        def _():
            wait_bytes(sem, k, buf.at[0:NATM])

    def side_wait(sem, k, buf):
        @pl.when(atmos)
        def _():
            wait_bytes(sem, k, buf.at[0, 0 : 3 * (NG - NATM)])

        @pl.when(ocean)
        def _():
            wait_bytes(sem, k, buf.at[0, 0 : 3 * NATM])

    def gather_send(k, sent, ev):
        each_partner(lambda p, d: remote(k, sent, ev.at[me], (d, t)).start())

    def slots_send(k, snd, rcv):
        for d in tiles:
            remote(k, snd.at[:, d], rcv.at[:, t], (g, d)).start()
        rcv[:, t] = snd[:, t]

    lane = lax.broadcasted_iota(I32, (LEV, COLS), 1)

    def laplace(w, r):
        mid = w[r]
        west = jnp.where(lane == 0, 0.0, pltpu.roll(mid, 1, 1))
        east = jnp.where(lane == COLS - 1, 0.0, pltpu.roll(mid, COLS - 1, 1))
        return w[r + 1] + w[r - 1] + east + west - 4.0 * mid

    def mix_row(x, r, cols):
        parts = []
        for c in range(3):
            ls = slice(c * 128, (c + 1) * 128)
            acc = cols[0] * x[r, 0:1, ls]
            for m in range(1, LEV):
                acc = acc + cols[m] * x[r, m : m + 1, ls]
            parts.append(acc)
        return jnp.concatenate(parts, axis=1)

    def forward_pair(f, ta, tb_row, put):
        for r in range(6):
            wa[r] = sp[r] * f[r]
        for r in range(1, 5):
            xa[r] = f[r] + SPREAD * sp[r] * laplace(wa, r)
        for r in range(1, 5):
            row = ta[r] * mix_row(xa, r, mb)
            ya[r] = row
            wb[r] = sp[r] * row
        for r in (2, 3):
            xa[r] = ya[r] + SPREAD * sp[r] * laplace(wb, r)
        for r in (2, 3):
            put(r, tb_row(r) * mix_row(xa, r, mb))

    def adjoint_pair(u, ta):
        for r in range(6):
            wa[r] = sp[r] * u[r]
        for r in range(1, 5):
            xa[r] = ta[r] * (u[r] + SPREAD * sp[r] * laplace(wa, r))
        for r in range(1, 5):
            row = mix_row(xa, r, mtb)
            ya[r] = row
            wb[r] = sp[r] * row
        for r in (2, 3):
            adj[r] = ya[r] + SPREAD * sp[r] * laplace(wb, r)

    def surface_rows(ref):
        return [ref[r, 0:1, c * 128 : (c + 1) * 128] for r in (2, 3) for c in range(3)]

    def put_surface(sent, ref):
        for h, row in enumerate(surface_rows(ref)):
            sent[h : h + 1, :] = row

    def put_masked():
        for h, row in enumerate(surface_rows(adj)):
            mtab[h : h + 1, :] = row * seat[h : h + 1, :]

    half = lax.broadcasted_iota(I32, (8, 128), 1) < CAP

    def pick(table, lo):
        return jnp.take_along_axis(table, lo, axis=1, mode="promise_in_bounds")

    def gather_adjoint():
        def body(i, carry):
            rows = pl.ds(pl.multiple_of(i * 8, 8), 8)
            lo, hi = slo[rows, :], shi[rows, :]
            out = jnp.zeros((8, 128), F32)
            for h in range(HI):
                table = jnp.broadcast_to(mtab[h : h + 1, :], (8, 128))
                out = jnp.where(hi == h, pick(table, lo), out)
            val[pl.ds(pl.multiple_of(i * 8 + 8, 8), 8), :] = out
            return carry

        lax.fori_loop(0, BLOCKS, body, 0, unroll=4)

    def gather_forward(ev):
        def body(i, carry):
            rows = pl.ds(pl.multiple_of(i * 8, 8), 8)
            lo, hi, owner = slo[rows, :], shi[rows, :], gi[rows, :]
            out = jnp.zeros((8, 128), F32)
            for h in range(HI):
                table = jnp.broadcast_to(ev[0, h : h + 1, :], (8, 128))
                for s in range(1, NATM):
                    table = jnp.where(owner == s, ev[s, h : h + 1, :], table)
                out = jnp.where(hi == h, pick(table, lo), out)
            here = pl.ds(pl.multiple_of(i * 8 + 8, 8), 8)
            val[here, :] = jnp.where(half, out, val[here, :]) * wv[rows, :]
            return carry

        lax.fori_loop(0, BLOCKS, body, 0, unroll=4)

    def put_slots(snd):
        own, beside = snd.at[0].reshape(NT, 128), snd.at[1].reshape(NT, 128)
        own[...] = val[8 : 8 + NT, :]
        beside[...] = jnp.where(
            lax.broadcasted_iota(I32, (NT, 128), 1) < CAP,
            val[7 : 7 + NT, :], pltpu.roll(val[9 : 9 + NT, :], CAP, 1),
        )

    def scatter(rcv, factor, index, hot, count):
        row_id = lax.broadcasted_iota(I32, (count, 128), 0)

        def body(i, acc):
            rows = pl.ds(pl.multiple_of(i * 8, 8), 8)
            v = rcv.reshape(NT, 128)[rows, :]
            if factor is not None:
                v = v * factor[rows, :]
            where = index[rows, :]
            top = v.astype(BF16).astype(F32)
            rest = v - top
            mid = rest.astype(BF16).astype(F32)
            low = rest - mid
            blocks = []
            for j in range(8):
                hit = row_id == where[j : j + 1, :]
                blocks.append(
                    jnp.concatenate([jnp.where(hit, p[j : j + 1, :], 0.0) for p in (top, mid, low)], axis=0).astype(BF16)
                )
            m = jnp.concatenate(blocks, axis=1)
            return acc + lax.dot_general(m, hot[i], (((1,), (1,)), ((), ())), preferred_element_type=F32)

        acc = lax.fori_loop(0, BLOCKS, body, jnp.zeros((3 * count, 128), F32), unroll=BLOCKS)
        return acc[0:count] + acc[count : 2 * count] + acc[2 * count : 3 * count]

    def scatter_own(rcv):
        return scatter(rcv.at[0], rw, rrow, onehot, 48)

    def scatter_beside(rcv):
        return scatter(rcv.at[1], None, rrowh, onehot_h, 16)

    def put_terms(total, ts):
        for p in range(NATM):
            ts[p, 0:HI, :] = total[8 + p * HI : 8 + (p + 1) * HI, :]

    def add_forcing(f, own, beside):
        for r in range(6):
            part = beside if r in (0, 1, 4, 5) else own
            first = {0: 0, 1: 3, 2: 0, 3: 3, 4: 8, 5: 11}[r]
            for c in range(3):
                ls = slice(c * 128, (c + 1) * 128)
                f[r, 0:1, ls] = f[r, 0:1, ls] + part[first + c : first + c + 1, :] * st[r, 1:2, ls]

    def term_sum(slots):
        total = slots[0] + slots[1]
        for p in range(2, NATM):
            total = total + jnp.where(ocean, slots[p], 0.0)
        return total

    for m in range(LEV):
        row = mix_ref[m]
        diag = lax.broadcasted_iota(I32, (LEV, LEV), 0) == lax.broadcasted_iota(I32, (LEV, LEV), 1)
        column = jnp.sum(jnp.where(diag, row, 0.0), axis=1, keepdims=True)
        mtb[m] = jnp.broadcast_to(column, (LEV, 128))
        for n in range(LEV):
            mb[n, m : m + 1, :] = jnp.broadcast_to(row[:, n : n + 1], (1, 128))
    for r in (0, 1):
        f1[2 + r] = init_ref[:, r, :]
        sp[2 + r] = spread_ref[:, r, :]
        t2[2 + r] = traj_ref[2, :, r, :]
        own3[2 + r] = traj_ref[3, :, r, :]
        xa[2 + r] = own3[2 + r] * cot_ref[:, r, :]
        st[2 + r, 0:1, :] = traj_ref[1, 0, r : r + 1, :]
        st[2 + r, 1:2, :] = sea_ref[r : r + 1, :].astype(F32)
    for r in (2, 3):
        u1[r] = mix_row(xa, r, mtb)
    put_surface(ev1.at[NATM], f1)

    pl.semaphore_wait(barrier, NT - 1 + jnp.where(atmos, 3 * (NG - NATM), 3 * NATM))
    gather_send(S0, ev1.at[NATM], ev1)
    halo_send(SP, sp)
    halo_send(U1, u1)
    rim_send(T2, t2)
    halo_send(ST, st)
    remote(DN, dst_ref, dn.at[0], (g, right)).start()
    remote(DN, dst_ref, dn.at[1], (g, left)).start()

    for r in (0, 1):
        t0[2 + r] = traj_ref[0, :, r, :]
        own1[2 + r] = traj_ref[1, :, r, :]
    for h in range(HI):
        seat[h : h + 1, :] = st[2 + h // 3, 1:2, (h % 3) * 128 : (h % 3 + 1) * 128]
    live = lax.broadcasted_iota(I32, (CAP, NT), 0) < cnt_ref[...]
    weight = jnp.where(live, w_ref[...], 0.0)
    ones = jnp.ones((CAP, NT), F32)
    wv[...] = jnp.concatenate([weight, ones], axis=0).T
    rw[...] = jnp.concatenate([ones, weight], axis=0).T
    srcc, dstc = srcc_ref[...], dst_ref[...]
    srcg = srcg_ref[...] - jnp.where(atmos, NATM, 0)
    gi[...] = jnp.concatenate([srcg, srcg], axis=0).T
    send_cell = jnp.concatenate([srcc, dstc], axis=0).T
    slo[...] = jnp.bitwise_and(send_cell, 127)
    shi[...] = jnp.right_shift(send_cell, 7)
    rlo[...] = jnp.bitwise_and(jnp.concatenate([dstc, srcc], axis=0), 127).T
    rrow[...] = jnp.concatenate([jnp.right_shift(dstc, 7), 8 + HI * srcg + jnp.right_shift(srcc, 7)], axis=0).T
    val[0:8, :] = jnp.zeros((8, 128), F32)
    val[8 + NT : 16 + NT, :] = jnp.zeros((8, 128), F32)

    wait_bytes(rsem, SP, sp.at[0:4])
    wait_bytes(rsem, U1, u1.at[0:4])
    wait_bytes(rsem, T2, t2.at[0:2])
    sp[0:2] = jnp.where(t > 0, sp[0:2], 0.0)
    sp[4:6] = jnp.where(t < NT - 1, sp[4:6], 0.0)
    halo_send(F1, f1)
    rim_send(T0, t0)
    adjoint_pair(u1, t2)
    put_masked()
    gather_adjoint()
    partner_wait(rsem, S0, ev1)
    gather_forward(ev1)
    put_slots(snd1)
    slots_send(A1, snd1, rcv1)

    for r in (2, 3):
        xa[r] = own1[r] * adj[r]
    for r in (2, 3):
        u2[r] = mix_row(xa, r, mtb)
    halo_send(U2, u2)

    wait_bytes(rsem, DN, dn)
    nearby = jnp.concatenate([dn[0], dn[1]], axis=0)
    rloh[...] = jnp.bitwise_and(nearby, 127).T
    rrowh[...] = (
        jnp.right_shift(nearby, 7) + jnp.where(lax.broadcasted_iota(I32, (2 * CAP, NT), 0) < CAP, 0, 8)
    ).T
    cell = lax.broadcasted_iota(I32, (128, 128), 0)

    @pl.loop(0, BLOCKS)
    def _(i):
        block = pl.ds(pl.multiple_of(i * 8, 8), 8)
        for index, hot in ((rlo, onehot), (rloh, onehot_h)):
            rows = index[block, :]
            for j in range(8):
                hit = jnp.where(cell == rows[j : j + 1, :], 1.0, 0.0).astype(BF16)
                hot[i, :, j * 128 : (j + 1) * 128] = hit

    wait_bytes(rsem, F1, f1.at[0:4])
    wait_bytes(rsem, T0, t0.at[0:2])
    wait_bytes(rsem, ST, st.at[0:4])
    wait_bytes(rsem, U2, u2.at[0:4])
    wait_bytes(ssem, F1, f1.at[0:4])
    wait_bytes(ssem, U2, u2.at[0:4])
    wait_bytes(rsem, A1, rcv1.at[:, 0 : NT - 1])
    own = scatter_own(rcv1)
    put_terms(own, ts1)
    each_partner(
        lambda p, d: [remote(TB1, ts1.at[p], tr1.at[2 - k, me], (d, s)).start() for k, s in enumerate(sides)]
    )
    add_forcing(f1, own, scatter_beside(rcv1))
    forward_pair(f1, t0, lambda r: own1[r], lambda r, value: f2.__setitem__(r, value))
    put_surface(ev2.at[NATM], f2)
    gather_send(S1, ev2.at[NATM], ev2)
    halo_send(F2, f2)

    side_wait(rsem, TB1, tr1.reshape(1, 3 * NATM, 8, 128))
    for k in range(3):
        part = term_sum(tr1.at[k])
        for i in range(2):
            r = 2 * k + i
            for c in range(3):
                ls = slice(c * 128, (c + 1) * 128)
                q = part[3 * i + c : 3 * i + c + 1, :] * st[r, 0:1, ls]
                u2[r, :, ls] = u2[r, :, ls] + mtb[0] * q
    adjoint_pair(u2, t0)
    put_masked()
    gather_adjoint()
    partner_wait(rsem, S1, ev2)
    gather_forward(ev2)
    put_slots(snd2)
    slots_send(A2, snd2, rcv2)

    wait_bytes(rsem, F2, f2.at[0:4])
    wait_bytes(ssem, F2, f2.at[0:4])
    partner_wait(ssem, S0, ev1)
    partner_wait(ssem, S1, ev2)
    side_wait(ssem, TB1, tr1.reshape(1, 3 * NATM, 8, 128))
    wait_bytes(ssem, A1, rcv1.at[:, 0 : NT - 1])
    wait_bytes(ssem, SP, sp.at[0:4])
    wait_bytes(ssem, U1, u1.at[0:4])
    wait_bytes(ssem, T2, t2.at[0:2])
    wait_bytes(ssem, T0, t0.at[0:2])
    wait_bytes(ssem, ST, st.at[0:4])
    wait_bytes(ssem, DN, dn)

    wait_bytes(rsem, A2, rcv2.at[:, 0 : NT - 1])
    own = scatter_own(rcv2)
    put_terms(own, ts2)
    each_partner(lambda p, d: remote(TB2, ts2.at[p], tr2.at[me], (d, t)).start())
    add_forcing(f2, own, scatter_beside(rcv2))
    forward_pair(f2, t2, lambda r: own3[r], lambda r, value: outf_ref.__setitem__((slice(None), r - 2, slice(None)), value))
    partner_wait(rsem, TB2, tr2)
    part = term_sum(tr2)
    for h in range(HI):
        ls = slice((h % 3) * 128, (h % 3 + 1) * 128)
        adj[2 + h // 3, 0:1, ls] = adj[2 + h // 3, 0:1, ls] + part[h : h + 1, :]
    for r in (2, 3):
        outg_ref[:, r - 2, :] = adj[r]
    wait_bytes(ssem, A2, rcv2.at[:, 0 : NT - 1])
    partner_wait(ssem, TB2, tr2)


def per_device(
    initial, cotangent, spread_coef, trajectory, mixing, sea_mask, src_group, src_cell, weight, counts, dst_cell
):
    vmem = lambda *shape, dtype=F32: pltpu.VMEM(shape, dtype)
    field = vmem(6, LEV, COLS)
    final, gradient = pl.pallas_call(
        kernel,
        out_shape=[jax.ShapeDtypeStruct((LEV, 2, COLS), F32)] * 2,
        in_specs=[pl.BlockSpec(memory_space=pltpu.VMEM)] * 11,
        out_specs=[pl.BlockSpec(memory_space=pltpu.VMEM)] * 2,
        scratch_shapes=[field] * 14
        + [vmem(6, 2, COLS), vmem(2, CAP, NT, dtype=I32)]
        + [vmem(NATM + 1, 8, 128)] * 2
        + [vmem(NATM, 8, 128)] * 2
        + [vmem(3, NATM, 8, 128), vmem(NATM, 8, 128)]
        + [vmem(2, NT, 1, 128)] * 4
        + [vmem(LEV, LEV, 128)] * 2
        + [vmem(8, 128)] * 2
        + [vmem(NT, 128, dtype=I32)] * 7
        + [vmem(NT, 128)] * 2
        + [vmem(NT + 16, 128)]
        + [vmem(BLOCKS, 128, 1024, dtype=BF16)] * 2
        + [pltpu.SemaphoreType.DMA((15,))] * 2,
        compiler_params=pltpu.CompilerParams(
            collective_id=0, has_side_effects=True, vmem_limit_bytes=40 * 1024 * 1024
        ),
    )(
        initial[0], cotangent[0], spread_coef[0], trajectory[:, 0], jnp.transpose(mixing, (1, 0, 2)), sea_mask[0],
        src_group[0, 0].T, src_cell[0, 0].T, weight[0, 0].T, counts[0], dst_cell[0, 0].T,
    )
    return final[None], gradient[None]


def solution(mesh):
    return jax.shard_map(
        per_device,
        mesh=mesh,
        in_specs=(
            P("comp", None, "tile", None),
            P("comp", None, "tile", None),
            P("comp", None, "tile", None),
            P(None, "comp", None, "tile", None),
            P("comp", None, None),
            P("comp", "tile", None),
            P("comp", "tile", None, None),
            P("comp", "tile", None, None),
            P("comp", "tile", None, None),
            P("comp", "tile", None),
            P("comp", "tile", None, None),
        ),
        out_specs=(P("comp", None, "tile", None), P("comp", None, "tile", None)),
        check_vma=False,
    )
```

```python
import functools

import jax
import jax.numpy as jnp
from jax import lax
from jax.experimental import pallas as pl
from jax.experimental.pallas import tpu as pltpu
from jax.sharding import PartitionSpec as P

MESH = pl.DeviceIdType.MESH
SPREAD = 0.12
NG, NATM, NT, LEV, COLS, CAP = 8, 6, 96, 12, 384, 64
NY, NZ = 8, 12
HI = 6
BLOCKS = NT // 8
F32, BF16, I32 = jnp.float32, jnp.bfloat16, jnp.int32

LOAD_ORDER = (4, 1, 3, 2, 0, 5, 9, 10, 7, 6, 8)
EDGE, FIRST, BACK, NEXT, DN, TS, S0, A0, TO = 0, 1, 2, 3, 4, 5, 6, 8, 10


def kernel(*refs):
    sources, out_ref, held, rest = refs[:11], refs[11], refs[12:23], refs[23:]
    init_ref, cot_ref, spread_ref, traj_ref, mix_ref, sea_ref, srcg_ref, srcc_ref, w_ref, cnt_ref, dst_ref = held
    (
        f, u, te, to, sp, wa, xa, ya, wb, adj, st,
        edge_s, edge_r, first_s, first_r, back_s, back_r, next_s, next_r, dn,
        ev, ts, tro, trs, snd, rcv,
        mat, mb, mtb, seat, mtab, gi, slo, shi, wv, val, alo, arow, aw, va, flo, frow, vf, hot_a, hot_f,
        ssem, rsem, isem,
    ) = rest
    g = lax.axis_index("comp")
    t = lax.axis_index("tile")
    y, z = t // NZ, lax.rem(t, NZ)
    right, left = lax.rem(t + 1, NT), lax.rem(t + NT - 1, NT)
    atmos = g < NATM
    ocean = g >= NATM
    me = jnp.where(atmos, g, g - NATM)

    def each_partner(act):
        @pl.when(atmos)
        def _():
            for p in range(NG - NATM):
                act(p, NATM + p)

        @pl.when(ocean)
        def _():
            for p in range(NATM):
                act(p, p)

    ys = [lax.rem(y + a, NY) * NZ for a in (4, 3, 5, 2, 6, 1, 7, 0)]

    def each_tile(act):
        @pl.loop(0, NZ - 1)
        def _(m):
            b = NZ // 2 + (1 - 2 * lax.rem(m, 2)) * ((m + 1) // 2)
            other = lax.rem(z + b, NZ)
            for row in ys:
                act(row + other)

        for row in ys[:-1]:
            act(row + z)

    barrier = pltpu.get_barrier_semaphore()

    def greet(dev):
        pl.semaphore_signal(barrier, inc=1, device_id=dev, device_id_type=MESH)

    loads = [pltpu.make_async_copy(a, b, isem.at[n]) for n, (a, b) in enumerate(zip(sources, held))]
    for n in LOAD_ORDER:
        loads[n].start()
    each_partner(lambda p, d: [greet((d, s)) for s in (t, left, right)])
    each_tile(lambda d: greet((g, d)))

    def remote(k, src, dst, dev):
        return pltpu.make_async_remote_copy(
            src_ref=src, dst_ref=dst, send_sem=ssem.at[k], recv_sem=rsem.at[k], device_id=dev, device_id_type=MESH
        )

    def beside_send(k, to_left, to_right, landing):
        remote(k, to_right, landing.at[0], (g, right)).start()
        remote(k, to_left, landing.at[1], (g, left)).start()

    def wait_bytes(sem, k, ref):
        pltpu.make_async_copy(ref, ref, sem.at[k]).wait()

    def partner_wait(sem, k, buf):
        @pl.when(atmos)
        def _():
            wait_bytes(sem, k, buf.at[0 : NG - NATM])

        @pl.when(ocean)
        def _():
            wait_bytes(sem, k, buf.at[0:NATM])

    def sides_wait(sem):
        slots = trs.reshape(1, 2 * NATM, 8, 128)

        @pl.when(atmos)
        def _():
            wait_bytes(sem, TS, slots.at[0, 0 : 2 * (NG - NATM)])

        @pl.when(ocean)
        def _():
            wait_bytes(sem, TS, slots.at[0])

    def surface_send(i):
        each_partner(lambda p, d: remote(S0 + i, ev.at[i, NATM], ev.at[i, me], (d, t)).start())

    lane = lax.broadcasted_iota(I32, (LEV, COLS), 1)

    def laplace(w, r):
        mid = w[r]
        west = jnp.where(lane == 0, 0.0, pltpu.roll(mid, 1, 1))
        east = jnp.where(lane == COLS - 1, 0.0, pltpu.roll(mid, COLS - 1, 1))
        return w[r + 1] + w[r - 1] + east + west - 4.0 * mid

    def mix_row(x, r, cols):
        parts = []
        for c in range(3):
            ls = slice(c * 128, (c + 1) * 128)
            acc = cols[0] * x[r, 0:1, ls]
            for m in range(1, LEV):
                acc = acc + cols[m] * x[r, m : m + 1, ls]
            parts.append(acc)
        return jnp.concatenate(parts, axis=1)

    def forward_pair(i):
        for r in range(6):
            wa[r] = sp[r] * f[i, r]
        for r in range(1, 5):
            xa[r] = f[i, r] + SPREAD * sp[r] * laplace(wa, r)
        for r in range(1, 5):
            row = te[i, r] * mix_row(xa, r, mb)
            ya[r] = row
            wb[r] = sp[r] * row
        for r in (2, 3):
            xa[r] = ya[r] + SPREAD * sp[r] * laplace(wb, r)
        for r in (2, 3):
            f[i + 1, r] = to[i, r] * mix_row(xa, r, mb)

    def adjoint_pair(i):
        for r in range(6):
            wa[r] = sp[r] * u[i, r]
        for r in range(1, 5):
            xa[r] = te[1 - i, r] * (u[i, r] + SPREAD * sp[r] * laplace(wa, r))
        for r in range(1, 5):
            row = mix_row(xa, r, mtb)
            ya[r] = row
            wb[r] = sp[r] * row
        for r in (2, 3):
            adj[r] = ya[r] + SPREAD * sp[r] * laplace(wb, r)

    def pack(dst, rows):
        at = 0
        for row in rows:
            dst[at : at + row.shape[0], :] = row
            at += row.shape[0]

    def surface_rows(strip):
        return [strip[r, 0:1, c * 128 : (c + 1) * 128] for r in (2, 3) for c in range(3)]

    def put_surface(i):
        for h, row in enumerate(surface_rows(f.at[i])):
            ev[i, NATM, h : h + 1, :] = row

    def put_masked():
        for h, row in enumerate(surface_rows(adj)):
            mtab[h : h + 1, :] = row * seat[h : h + 1, :]

    def first_half(rows):
        return lax.broadcasted_iota(I32, (rows, 128), 1) < CAP

    def pick(table, lo):
        return jnp.take_along_axis(table, lo, axis=1, mode="promise_in_bounds")

    def gather_adjoint():
        def body(i, carry):
            rows = pl.ds(pl.multiple_of(i * 8, 8), 8)
            lo, hi = slo[rows, :], shi[rows, :]
            out = jnp.zeros((8, 128), F32)
            for h in range(HI):
                table = jnp.broadcast_to(mtab[h : h + 1, :], (8, 128))
                out = jnp.where(hi == h, pick(table, lo), out)
            val[pl.ds(pl.multiple_of(i * 8 + 8, 8), 8), :] = out
            return carry

        lax.fori_loop(0, BLOCKS, body, 0, unroll=4)

    def gather_forward(owners):
        def body(i, carry):
            rows = pl.ds(pl.multiple_of(i * 8, 8), 8)
            lo, hi, owner = slo[rows, :], shi[rows, :], gi[rows, :]
            out = jnp.zeros((8, 128), F32)
            for h in range(HI):
                table = jnp.broadcast_to(owners[0, h : h + 1, :], (8, 128))
                for s in range(1, NATM):
                    table = jnp.where(owner == s, owners[s, h : h + 1, :], table)
                out = jnp.where(hi == h, pick(table, lo), out)
            here = pl.ds(pl.multiple_of(i * 8 + 8, 8), 8)
            val[here, :] = jnp.where(first_half(8), out, val[here, :]) * wv[rows, :]
            return carry

        lax.fori_loop(0, BLOCKS, body, 0, unroll=4)

    def send_slots(i):
        own, beside = snd.at[i, 0].reshape(NT, 128), snd.at[i, 1].reshape(NT, 128)
        own[...] = val[8 : 8 + NT, :]
        beside[...] = jnp.where(first_half(NT), val[7 : 7 + NT, :], pltpu.roll(val[9 : 9 + NT, :], CAP, 1))
        each_tile(lambda d: remote(A0 + i, snd.at[i, :, d], rcv.at[i, :, t], (g, d)).start())
        rcv[i, :, t] = snd[i, :, t]

    def packed(x):
        return jnp.where(first_half(NT // 2), x[0 : NT // 2], x[NT // 2 : NT])

    def scatter(value, index, hot, blocks, count, unroll):
        row_id = lax.broadcasted_iota(I32, (count, 128), 0)

        def body(i, acc):
            rows = pl.ds(pl.multiple_of(i * 8, 8), 8)
            v, where = value[rows, :], index[rows, :]
            top = v.astype(BF16).astype(F32)
            rest = v - top
            mid = rest.astype(BF16).astype(F32)
            low = rest - mid
            parts = []
            for j in range(8):
                hit = row_id == where[j : j + 1, :]
                parts.append(
                    jnp.concatenate([jnp.where(hit, p[j : j + 1, :], 0.0) for p in (top, mid, low)], axis=0).astype(BF16)
                )
            m = jnp.concatenate(parts, axis=1)
            return acc + lax.dot_general(m, hot[i], (((1,), (1,)), ((), ())), preferred_element_type=F32)

        acc = lax.fori_loop(0, blocks, body, jnp.zeros((3 * count, 128), F32), unroll=unroll)
        return acc[0:count] + acc[count : 2 * count] + acc[2 * count : 3 * count]

    def scatter_adjoint(i):
        got = rcv.at[i, 0].reshape(NT, 128)[...]
        va[...] = jnp.where(first_half(NT // 2), pltpu.roll(got[0 : NT // 2], CAP, 1), got[NT // 2 : NT]) * aw[...]
        total = scatter(va, arow, hot_a, BLOCKS // 2, 40, 6)
        for p in range(NATM):
            ts[i, p, 0:HI, :] = total[p * HI : (p + 1) * HI, :]

    def scatter_forward(i):
        got = rcv.at[i, 0].reshape(NT, 128)[...]
        vf[0 : NT // 2, :] = jnp.where(first_half(NT // 2), got[0 : NT // 2], pltpu.roll(got[NT // 2 : NT], CAP, 1))
        vf[NT // 2 :, :] = rcv.at[i, 1].reshape(NT, 128)[...]
        total = scatter(vf, frow, hot_f, 3 * BLOCKS // 2, 24, 6)
        for r in range(6):
            first = (8, 11, 0, 3, 16, 19)[r]
            for c in range(3):
                ls = slice(c * 128, (c + 1) * 128)
                f[i, r, 0:1, ls] = f[i, r, 0:1, ls] + total[first + c : first + c + 1, :] * st[r, 1:2, ls]

    def term_sum(slots):
        total = slots[0] + slots[1]
        for p in range(2, NATM):
            total = total + jnp.where(ocean, slots[p], 0.0)
        return total

    def put_hot(index, hot, start, stop):
        cell = lax.broadcasted_iota(I32, (128, 128), 0)

        @pl.loop(start, stop)
        def _(i):
            rows = index[pl.ds(pl.multiple_of(i * 8, 8), 8), :]
            for j in range(8):
                hit = jnp.where(cell == rows[j : j + 1, :], 1.0, 0.0).astype(BF16)
                hot[i, :, j * 128 : (j + 1) * 128] = hit

    for n in LOAD_ORDER[:6]:
        loads[n].wait()
    diag = lax.broadcasted_iota(I32, (LEV, LEV), 0) == lax.broadcasted_iota(I32, (LEV, LEV), 1)
    for m in range(LEV):
        row = mix_ref[m]
        mat[m : m + 1, :] = row
        mtb[m] = jnp.broadcast_to(jnp.sum(jnp.where(diag, row, 0.0), axis=1, keepdims=True), (LEV, 128))
    for n in range(LEV):
        mb[n] = jnp.broadcast_to(mat[:, n : n + 1], (LEV, 128))
    for r in (0, 1):
        f[0, 2 + r] = init_ref[:, r, :]
        sp[2 + r] = spread_ref[:, r, :]
        te[0, 2 + r] = traj_ref[0, :, r, :]
        te[1, 2 + r] = traj_ref[2, :, r, :]
        to[0, 2 + r] = traj_ref[1, :, r, :]
        to[1, 2 + r] = traj_ref[3, :, r, :]
        xa[2 + r] = to[1, 2 + r] * cot_ref[:, r, :]
        st[2 + r, 0:1, :] = traj_ref[1, 0, r : r + 1, :]
        st[2 + r, 1:2, :] = sea_ref[r : r + 1, :].astype(F32)
    for r in (2, 3):
        u[0, r] = mix_row(xa, r, mtb)
    put_surface(0)
    for side, near in ((0, 2), (1, 3)):
        pack(edge_s.at[side], [sp[2], sp[3], u[0, 2], u[0, 3], te[1, near], st[2], st[3]])
        pack(first_s.at[side], [f[0, 2], f[0, 3], te[0, near]])

    pl.semaphore_wait(barrier, NT - 1 + jnp.where(atmos, 3 * (NG - NATM), 3 * NATM))
    beside_send(EDGE, edge_s.at[0], edge_s.at[1], edge_r)
    surface_send(0)

    for n in LOAD_ORDER[6:]:
        loads[n].wait()
    for h in range(HI):
        seat[h : h + 1, :] = st[2 + h // 3, 1:2, (h % 3) * 128 : (h % 3 + 1) * 128]
    live = lax.broadcasted_iota(I32, (CAP, NT), 0) < cnt_ref[...]
    weight = jnp.where(live, w_ref[...], 0.0)
    wv[...] = jnp.concatenate([weight, jnp.ones((CAP, NT), F32)], axis=0).T
    aw[...] = packed(jnp.concatenate([weight, weight], axis=0).T)
    srcc, dstc = srcc_ref[...], dst_ref[...]
    srcg = srcg_ref[...] - jnp.where(atmos, NATM, 0)
    gi[...] = jnp.concatenate([srcg, srcg], axis=0).T
    send_cell = jnp.concatenate([srcc, dstc], axis=0).T
    slo[...] = jnp.bitwise_and(send_cell, 127)
    shi[...] = jnp.right_shift(send_cell, 7)
    come = packed(jnp.concatenate([srcc, srcc], axis=0).T)
    alo[...] = jnp.bitwise_and(come, 127)
    arow[...] = HI * packed(gi[...]) + jnp.right_shift(come, 7)
    come = packed(jnp.concatenate([dstc, dstc], axis=0).T)
    flo[0 : NT // 2, :] = jnp.bitwise_and(come, 127)
    frow[0 : NT // 2, :] = jnp.right_shift(come, 7)
    val[0:8, :] = jnp.zeros((8, 128), F32)
    val[8 + NT : 16 + NT, :] = jnp.zeros((8, 128), F32)

    wait_bytes(rsem, EDGE, edge_r)
    beside_send(FIRST, first_s.at[0], first_s.at[1], first_r)
    for side, rows, near, inside in ((0, (0, 1), 1, t > 0), (1, (4, 5), 4, t < NT - 1)):
        got = edge_r.at[side]
        for k, r in enumerate(rows):
            sp[r] = jnp.where(inside, got[k * LEV : (k + 1) * LEV, :], 0.0)
            u[0, r] = got[(2 + k) * LEV : (3 + k) * LEV, :]
            st[r] = got[5 * LEV + 2 * k : 5 * LEV + 2 * k + 2, :]
        te[1, near] = got[4 * LEV : 5 * LEV, :]

    def unpack_pair(buf, i, landing):
        for side, rows in ((0, (0, 1)), (1, (4, 5))):
            for k, r in enumerate(rows):
                buf[i, r] = landing[side, k * LEV : (k + 1) * LEV, :]

    @pl.loop(0, 2)
    def _(i):
        adjoint_pair(i)
        put_masked()
        gather_adjoint()
        partner_wait(rsem, S0 + i, ev.at[i])
        gather_forward(ev.at[i])
        send_slots(i)

        @pl.when(i == 0)
        def _():
            for r in (2, 3):
                xa[r] = to[0, r] * adj[r]
            for r in (2, 3):
                u[1, r] = mix_row(xa, r, mtb)
            pack(back_s, [u[1, 2], u[1, 3]])
            beside_send(DN, dst_ref, dst_ref, dn)
            beside_send(BACK, back_s, back_s, back_r)
            put_hot(alo, hot_a, 0, BLOCKS // 2)
            put_hot(flo, hot_f, 0, BLOCKS // 2)
            wait_bytes(rsem, FIRST, first_r)
            unpack_pair(f, 0, first_r)
            te[0, 1] = first_r[0, 2 * LEV : 3 * LEV, :]
            te[0, 4] = first_r[1, 2 * LEV : 3 * LEV, :]
            wait_bytes(rsem, DN, dn)
            nearby = jnp.concatenate([dn[0], dn[1]], axis=0).T
            flo[NT // 2 :, :] = jnp.bitwise_and(nearby, 127)
            frow[NT // 2 :, :] = jnp.right_shift(nearby, 7) + jnp.where(first_half(NT), 8, 16)
            put_hot(flo, hot_f, BLOCKS // 2, 3 * BLOCKS // 2)
            wait_bytes(rsem, BACK, back_r)
            unpack_pair(u, 1, back_r)

        @pl.when(i == 1)
        def _():
            beside_send(NEXT, next_s, next_s, next_r)
            for k, ref in ((EDGE, edge_s), (FIRST, first_s), (BACK, back_r), (DN, dn)):
                wait_bytes(ssem, k, ref)
            partner_wait(ssem, S0, ev.at[0])
            partner_wait(ssem, S0 + 1, ev.at[1])
            partner_wait(ssem, TO, tro.at[0])
            sides_wait(ssem)
            wait_bytes(ssem, A0, rcv.at[0, :, 0 : NT - 1])
            wait_bytes(rsem, NEXT, next_r)
            unpack_pair(f, 1, next_r)

        wait_bytes(rsem, A0 + i, rcv.at[i, :, 0 : NT - 1])
        scatter_adjoint(i)
        @pl.when(i == 0)
        def _():
            each_partner(
                lambda p, d: [
                    remote(TS, ts.at[0, p], trs.at[1, me], (d, left)).start(),
                    remote(TS, ts.at[0, p], trs.at[0, me], (d, right)).start(),
                ]
            )

        each_partner(lambda p, d: remote(TO + i, ts.at[i, p], tro.at[i, me], (d, t)).start())
        scatter_forward(i)
        forward_pair(i)

        @pl.when(i == 0)
        def _():
            put_surface(1)
            surface_send(1)
            pack(next_s, [f[1, 2], f[1, 3]])
            partner_wait(rsem, TO, tro.at[0])
            sides_wait(rsem)
            for k, slots in enumerate((trs.at[0], tro.at[0], trs.at[1])):
                part = term_sum(slots)
                for e in range(2):
                    r = 2 * k + e
                    for c in range(3):
                        ls = slice(c * 128, (c + 1) * 128)
                        q = part[3 * e + c : 3 * e + c + 1, :] * st[r, 0:1, ls]
                        u[1, r, :, ls] = u[1, r, :, ls] + mtb[0] * q

    for r in (2, 3):
        out_ref[0, :, r - 2, :] = f[2, r]
        out_ref[1, :, r - 2, :] = adj[r]
    wait_bytes(ssem, NEXT, next_r)
    wait_bytes(ssem, A0 + 1, rcv.at[1, :, 0 : NT - 1])
    partner_wait(rsem, TO + 1, tro.at[1])
    part = term_sum(tro.at[1])
    for h in range(HI):
        ls = slice((h % 3) * 128, (h % 3 + 1) * 128)
        out_ref[1, 0, h // 3 : h // 3 + 1, ls] = adj[2 + h // 3, 0:1, ls] + part[h : h + 1, :]
    partner_wait(ssem, TO + 1, tro.at[1])


def per_device(
    initial, cotangent, spread_coef, trajectory, mixing, sea_mask, src_group, src_cell, weight, counts, dst_cell
):
    vmem = lambda *shape, dtype=F32: pltpu.VMEM(shape, dtype)
    field = vmem(6, LEV, COLS)
    operands = (
        initial[0], cotangent[0], spread_coef[0], trajectory[:, 0], jnp.transpose(mixing, (1, 0, 2)), sea_mask[0],
        src_group[0, 0].T, src_cell[0, 0].T, weight[0, 0].T, counts[0], dst_cell[0, 0].T,
    )
    (both,) = pl.pallas_call(
        kernel,
        out_shape=[jax.ShapeDtypeStruct((2, LEV, 2, COLS), F32)],
        in_specs=[pl.BlockSpec(memory_space=pltpu.HBM)] * 11,
        out_specs=[pl.BlockSpec(memory_space=pltpu.VMEM)],
        scratch_shapes=[pltpu.VMEM(a.shape, a.dtype) for a in operands]
        + [vmem(3, 6, LEV, COLS), vmem(2, 6, LEV, COLS), vmem(2, 6, LEV, COLS), vmem(2, 6, LEV, COLS)]
        + [field] * 6
        + [vmem(6, 2, COLS)]
        + [vmem(2, 64, COLS)] * 2
        + [vmem(2, 40, COLS)] * 2
        + [vmem(24, COLS), vmem(2, 24, COLS)] * 2
        + [vmem(2, CAP, NT, dtype=I32)]
        + [vmem(2, NATM + 1, 8, 128)]
        + [vmem(2, NATM, 8, 128)] * 3
        + [vmem(2, 2, NT, 1, 128)] * 2
        + [vmem(LEV, LEV)]
        + [vmem(LEV, LEV, 128)] * 2
        + [vmem(8, 128)] * 2
        + [vmem(NT, 128, dtype=I32)] * 3
        + [vmem(NT, 128), vmem(NT + 16, 128)]
        + [vmem(NT // 2, 128, dtype=I32)] * 2
        + [vmem(NT // 2, 128)] * 2
        + [vmem(3 * NT // 2, 128, dtype=I32)] * 2
        + [vmem(3 * NT // 2, 128)]
        + [vmem(BLOCKS // 2, 128, 1024, dtype=BF16), vmem(3 * BLOCKS // 2, 128, 1024, dtype=BF16)]
        + [pltpu.SemaphoreType.DMA((12,))] * 2
        + [pltpu.SemaphoreType.DMA((11,))],
        compiler_params=pltpu.CompilerParams(
            collective_id=0, has_side_effects=True, vmem_limit_bytes=64 * 1024 * 1024
        ),
    )(*operands)
    return both[0:1], both[1:2]


def solution(mesh):
    return jax.shard_map(
        per_device,
        mesh=mesh,
        in_specs=(
            P("comp", None, "tile", None),
            P("comp", None, "tile", None),
            P("comp", None, "tile", None),
            P(None, "comp", None, "tile", None),
            P("comp", None, None),
            P("comp", "tile", None),
            P("comp", "tile", None, None),
            P("comp", "tile", None, None),
            P("comp", "tile", None, None),
            P("comp", "tile", None),
            P("comp", "tile", None, None),
        ),
        out_specs=(P("comp", None, "tile", None), P("comp", None, "tile", None)),
        check_vma=False,
    )
```

```python
import functools

import jax
import jax.numpy as jnp
from jax import lax
from jax.experimental import pallas as pl
from jax.experimental.pallas import tpu as pltpu
from jax.sharding import PartitionSpec as P

MESH = pl.DeviceIdType.MESH
SPREAD = 0.12
NG, NATM, NT, LEV, COLS, CAP = 8, 6, 96, 12, 384, 64
NY, NZ = 8, 12
HI = 6
BLOCKS = NT // 8
F32, BF16, I32 = jnp.float32, jnp.bfloat16, jnp.int32

LOAD_ORDER = (4, 1, 3, 2, 0, 5, 9, 10, 7, 6, 8)
EDGE, FIRST, BACK, NEXT, DN, TS, S0, A0, TO = 0, 1, 2, 3, 4, 5, 6, 8, 10


def tile_offsets():
    offsets = [(a, b) for a in range(NY) for b in range(NZ) if (a, b) != (0, 0)]
    return sorted(offsets, key=lambda o: -(min(o[0], NY - o[0]) + min(o[1], NZ - o[1])))


def kernel(*refs):
    sources, out_ref, held, rest = refs[:11], refs[11], refs[12:23], refs[23:]
    init_ref, cot_ref, spread_ref, traj_ref, mix_ref, sea_ref, srcg_ref, srcc_ref, w_ref, cnt_ref, dst_ref = held
    (
        f, u, te, to, sp, wa, xa, ya, wb, adj, st,
        edge_s, edge_r, first_s, first_r, back_s, back_r, next_s, next_r, dn,
        ev, ts, tro, trs, snd, rcv,
        mat, mb, mtb, seat, mtab, gi, slo, shi, wv, val, alo, arow, aw, va, cells, frow, vf, hot_a, hot_f,
        ssem, rsem, isem,
    ) = rest
    g = lax.axis_index("comp")
    t = lax.axis_index("tile")
    y, z = t // NZ, lax.rem(t, NZ)
    right, left = lax.rem(t + 1, NT), lax.rem(t + NT - 1, NT)
    atmos = g < NATM
    ocean = g >= NATM
    me = jnp.where(atmos, g, g - NATM)

    def each_partner(act):
        @pl.when(atmos)
        def _():
            for p in range(NG - NATM):
                act(p, NATM + p)

        @pl.when(ocean)
        def _():
            for p in range(NATM):
                act(p, p)

    ys = [lax.rem(y + a, NY) * NZ for a in range(NY)]
    zs = [lax.rem(z + b, NZ) for b in range(NZ)]
    tiles = [ys[a] + zs[b] for a, b in tile_offsets()]

    def each_tile(act):
        for d in tiles:
            act(d)

    barrier = pltpu.get_barrier_semaphore()

    def greet(dev):
        pl.semaphore_signal(barrier, inc=1, device_id=dev, device_id_type=MESH)

    loads = [pltpu.make_async_copy(a, b, isem.at[n]) for n, (a, b) in enumerate(zip(sources, held))]
    for n in LOAD_ORDER:
        loads[n].start()
    each_tile(lambda d: greet((g, d)))
    each_partner(lambda p, d: [greet((d, s)) for s in (left, right, t)])

    def remote(k, src, dst, dev):
        return pltpu.make_async_remote_copy(
            src_ref=src, dst_ref=dst, send_sem=ssem.at[k], recv_sem=rsem.at[k], device_id=dev, device_id_type=MESH
        )

    def beside_send(k, to_left, to_right, landing):
        remote(k, to_right, landing.at[0], (g, right)).start()
        remote(k, to_left, landing.at[1], (g, left)).start()

    def wait_bytes(sem, k, ref):
        pltpu.make_async_copy(ref, ref, sem.at[k]).wait()

    def partner_wait(sem, k, buf):
        @pl.when(atmos)
        def _():
            wait_bytes(sem, k, buf.at[0 : NG - NATM])

        @pl.when(ocean)
        def _():
            wait_bytes(sem, k, buf.at[0:NATM])

    def sides_wait(sem):
        slots = trs.reshape(1, 2 * NATM, 8, 128)

        @pl.when(atmos)
        def _():
            wait_bytes(sem, TS, slots.at[0, 0 : 2 * (NG - NATM)])

        @pl.when(ocean)
        def _():
            wait_bytes(sem, TS, slots.at[0])

    def surface_send(i):
        each_partner(lambda p, d: remote(S0 + i, ev.at[i, NATM], ev.at[i, me], (d, t)).start())

    lane = lax.broadcasted_iota(I32, (LEV, COLS), 1)

    def laplace(w, r):
        mid = w[r]
        west = jnp.where(lane == 0, 0.0, pltpu.roll(mid, 1, 1))
        east = jnp.where(lane == COLS - 1, 0.0, pltpu.roll(mid, COLS - 1, 1))
        return w[r + 1] + w[r - 1] + east + west - 4.0 * mid

    def mix_row(x, r, cols):
        parts = []
        for c in range(3):
            ls = slice(c * 128, (c + 1) * 128)
            acc = cols[0] * x[r, 0:1, ls]
            for m in range(1, LEV):
                acc = acc + cols[m] * x[r, m : m + 1, ls]
            parts.append(acc)
        return jnp.concatenate(parts, axis=1)

    def forward_pair(i):
        for r in range(6):
            wa[r] = sp[r] * f[i, r]
        for r in range(1, 5):
            xa[r] = f[i, r] + SPREAD * sp[r] * laplace(wa, r)
        for r in range(1, 5):
            row = te[i, r] * mix_row(xa, r, mb)
            ya[r] = row
            wb[r] = sp[r] * row
        for r in (2, 3):
            xa[r] = ya[r] + SPREAD * sp[r] * laplace(wb, r)
        for r in (2, 3):
            f[i + 1, r] = to[i, r] * mix_row(xa, r, mb)

    def adjoint_pair(i):
        for r in range(6):
            wa[r] = sp[r] * u[i, r]
        for r in range(1, 5):
            xa[r] = te[1 - i, r] * (u[i, r] + SPREAD * sp[r] * laplace(wa, r))
        for r in range(1, 5):
            row = mix_row(xa, r, mtb)
            ya[r] = row
            wb[r] = sp[r] * row
        for r in (2, 3):
            adj[r] = ya[r] + SPREAD * sp[r] * laplace(wb, r)

    def pack(dst, rows):
        at = 0
        for row in rows:
            dst[at : at + row.shape[0], :] = row
            at += row.shape[0]

    def surface_rows(strip):
        return [strip[r, 0:1, c * 128 : (c + 1) * 128] for r in (2, 3) for c in range(3)]

    def put_surface(i):
        for h, row in enumerate(surface_rows(f.at[i])):
            ev[i, NATM, h : h + 1, :] = row

    def put_masked():
        for h, row in enumerate(surface_rows(adj)):
            mtab[h : h + 1, :] = row * seat[h : h + 1, :]

    def first_half(rows):
        return lax.broadcasted_iota(I32, (rows, 128), 1) < CAP

    def pick(table, lo):
        return jnp.take_along_axis(table, lo, axis=1, mode="promise_in_bounds")

    def gather_adjoint():
        def body(i, carry):
            rows = pl.ds(pl.multiple_of(i * 8, 8), 8)
            lo, hi = slo[rows, :], shi[rows, :]
            out = jnp.zeros((8, 128), F32)
            for h in range(HI):
                table = jnp.broadcast_to(mtab[h : h + 1, :], (8, 128))
                out = jnp.where(hi == h, pick(table, lo), out)
            val[pl.ds(pl.multiple_of(i * 8 + 8, 8), 8), :] = out
            return carry

        lax.fori_loop(0, BLOCKS, body, 0, unroll=4)

    def gather_forward(owners):
        def body(i, carry):
            rows = pl.ds(pl.multiple_of(i * 8, 8), 8)
            lo, hi, owner = slo[rows, :], shi[rows, :], gi[rows, :]
            out = jnp.zeros((8, 128), F32)
            for h in range(HI):
                table = jnp.broadcast_to(owners[0, h : h + 1, :], (8, 128))
                for s in range(1, NATM):
                    table = jnp.where(owner == s, owners[s, h : h + 1, :], table)
                out = jnp.where(hi == h, pick(table, lo), out)
            here = pl.ds(pl.multiple_of(i * 8 + 8, 8), 8)
            val[here, :] = jnp.where(first_half(8), out, val[here, :]) * wv[rows, :]
            return carry

        lax.fori_loop(0, BLOCKS, body, 0, unroll=4)

    def send_slots(i):
        own, beside = snd.at[i, 0].reshape(NT, 128), snd.at[i, 1].reshape(NT, 128)
        own[...] = val[8 : 8 + NT, :]
        beside[...] = jnp.where(first_half(NT), val[7 : 7 + NT, :], pltpu.roll(val[9 : 9 + NT, :], CAP, 1))
        each_tile(lambda d: remote(A0 + i, snd.at[i, :, d], rcv.at[i, :, t], (g, d)).start())
        rcv[i, :, t] = snd[i, :, t]

    def packed(x):
        return jnp.where(first_half(NT // 2), x[0 : NT // 2], x[NT // 2 : NT])

    def scatter(value, index, hot, blocks, count, unroll, side):
        row_id = lax.broadcasted_iota(I32, (count, 128), 0)

        def body(i, acc):
            rows = pl.ds(pl.multiple_of(i * 8, 8), 8)
            v, where = value[rows, :], index[rows, :]
            top = v.astype(BF16).astype(F32)
            rest = v - top
            mid = rest.astype(BF16).astype(F32)
            low = rest - mid
            parts = []
            for j in range(8):
                hit = row_id == where[j : j + 1, :]
                parts.append(
                    jnp.concatenate([jnp.where(hit, p[j : j + 1, :], 0.0) for p in (top, mid, low)], axis=0).astype(BF16)
                )
            m = jnp.concatenate(parts, axis=1)
            return acc + lax.dot_general(m, hot[i], (((1,), (side,)), ((), ())), preferred_element_type=F32)

        acc = lax.fori_loop(0, blocks, body, jnp.zeros((3 * count, 128), F32), unroll=unroll)
        return acc[0:count] + acc[count : 2 * count] + acc[2 * count : 3 * count]

    def scatter_adjoint(i):
        got = rcv.at[i, 0].reshape(NT, 128)[...]
        va[...] = jnp.where(first_half(NT // 2), pltpu.roll(got[0 : NT // 2], CAP, 1), got[NT // 2 : NT]) * aw[...]
        total = scatter(va, arow, hot_a, BLOCKS // 2, 40, 6, 1)
        for p in range(NATM):
            ts[i, p, 0:HI, :] = total[p * HI : (p + 1) * HI, :]

    def scatter_forward(i):
        got = rcv.at[i, 0].reshape(NT, 128)[...]
        vf[0 : NT // 2, :] = jnp.where(first_half(NT // 2), got[0 : NT // 2], pltpu.roll(got[NT // 2 : NT], CAP, 1))
        vf[NT // 2 :, :] = rcv.at[i, 1].reshape(NT, 128)[...]
        total = scatter(vf, frow, hot_f, 3 * BLOCKS // 2, 24, 9, 0)
        for r in range(6):
            first = (8, 11, 0, 3, 16, 19)[r]
            for c in range(3):
                ls = slice(c * 128, (c + 1) * 128)
                f[i, r, 0:1, ls] = f[i, r, 0:1, ls] + total[first + c : first + c + 1, :] * st[r, 1:2, ls]

    def term_sum(slots):
        total = slots[0] + slots[1]
        for p in range(2, NATM):
            total = total + jnp.where(ocean, slots[p], 0.0)
        return total

    def put_hot(index, hot, start, stop):
        cell = lax.broadcasted_iota(I32, (128, 128), 0)

        @pl.loop(start, stop)
        def _(i):
            rows = index[pl.ds(pl.multiple_of(i * 8, 8), 8), :]
            for j in range(8):
                hit = jnp.where(cell == rows[j : j + 1, :], 1.0, 0.0).astype(BF16)
                hot[i, :, j * 128 : (j + 1) * 128] = hit

    def put_hot_columns(cells, start, count):
        target = lax.broadcasted_iota(I32, (128, 128), 1)

        @pl.loop(0, count)
        def _(i):
            columns = pltpu.roll(cells[...], lax.rem(128 - 8 * i, 128), 1)
            for j in range(8):
                hit = jnp.where(target == columns[:, j : j + 1], 1.0, 0.0).astype(BF16)
                hot_f[start + i, j * 128 : (j + 1) * 128, :] = hit

    for n in LOAD_ORDER[:6]:
        loads[n].wait()
    diag = lax.broadcasted_iota(I32, (LEV, LEV), 0) == lax.broadcasted_iota(I32, (LEV, LEV), 1)
    for m in range(LEV):
        row = mix_ref[m]
        mat[m : m + 1, :] = row
        mtb[m] = jnp.broadcast_to(jnp.sum(jnp.where(diag, row, 0.0), axis=1, keepdims=True), (LEV, 128))
    for n in range(LEV):
        mb[n] = jnp.broadcast_to(mat[:, n : n + 1], (LEV, 128))
    for r in (0, 1):
        f[0, 2 + r] = init_ref[:, r, :]
        sp[2 + r] = spread_ref[:, r, :]
        te[0, 2 + r] = traj_ref[0, :, r, :]
        te[1, 2 + r] = traj_ref[2, :, r, :]
        to[0, 2 + r] = traj_ref[1, :, r, :]
        to[1, 2 + r] = traj_ref[3, :, r, :]
        xa[2 + r] = to[1, 2 + r] * cot_ref[:, r, :]
        st[2 + r, 0:1, :] = traj_ref[1, 0, r : r + 1, :]
        st[2 + r, 1:2, :] = sea_ref[r : r + 1, :].astype(F32)
    for r in (2, 3):
        u[0, r] = mix_row(xa, r, mtb)
    put_surface(0)
    for side, near in ((0, 2), (1, 3)):
        far = 5 - near
        pack(edge_s.at[side], [sp[near], u[0, near], sp[far] * u[0, far], te[1, near]])
        pack(first_s.at[side], [f[0, 2], f[0, 3], te[0, near], sp[far], st[2], st[3]])

    pl.semaphore_wait(barrier, NT - 1 + jnp.where(atmos, 3 * (NG - NATM), 3 * NATM))
    beside_send(EDGE, edge_s.at[0], edge_s.at[1], edge_r)
    surface_send(0)

    for n in LOAD_ORDER[6:]:
        loads[n].wait()
    for h in range(HI):
        seat[h : h + 1, :] = st[2 + h // 3, 1:2, (h % 3) * 128 : (h % 3 + 1) * 128]
    live = lax.broadcasted_iota(I32, (CAP, NT), 0) < cnt_ref[...]
    weight = jnp.where(live, w_ref[...], 0.0)
    wv[...] = jnp.concatenate([weight, jnp.ones((CAP, NT), F32)], axis=0).T
    aw[...] = packed(jnp.concatenate([weight, weight], axis=0).T)
    srcc, dstc = srcc_ref[...], dst_ref[...]
    srcg = srcg_ref[...] - jnp.where(atmos, NATM, 0)
    gi[...] = jnp.concatenate([srcg, srcg], axis=0).T
    send_cell = jnp.concatenate([srcc, dstc], axis=0).T
    slo[...] = jnp.bitwise_and(send_cell, 127)
    shi[...] = jnp.right_shift(send_cell, 7)
    come = packed(jnp.concatenate([srcc, srcc], axis=0).T)
    alo[...] = jnp.bitwise_and(come, 127)
    arow[...] = HI * packed(gi[...]) + jnp.right_shift(come, 7)
    frow[0 : NT // 2, :] = jnp.right_shift(packed(jnp.concatenate([dstc, dstc], axis=0).T), 7)
    val[0:8, :] = jnp.zeros((8, 128), F32)
    val[8 + NT : 16 + NT, :] = jnp.zeros((8, 128), F32)

    beside_send(DN, dst_ref, dst_ref, dn)
    put_hot(alo, hot_a, 0, BLOCKS // 2)
    cells[0:CAP, 0 : NT // 2] = jnp.bitwise_and(dstc[:, 0 : NT // 2], 127)
    cells[CAP:, 0 : NT // 2] = jnp.bitwise_and(dstc[:, NT // 2 :], 127)
    put_hot_columns(cells, 0, BLOCKS // 2)

    wait_bytes(rsem, EDGE, edge_r)
    beside_send(FIRST, first_s.at[0], first_s.at[1], first_r)
    beyond = ((0, 1, 0, t > 0), (1, 4, 5, t < NT - 1))
    for side, near, far, inside in beyond:
        got = edge_r.at[side]
        sp[near] = jnp.where(inside, got[0:LEV, :], 0.0)
        u[0, near] = got[LEV : 2 * LEV, :]
        sp[far] = jnp.where(inside, jnp.ones((LEV, COLS), F32), 0.0)
        u[0, far] = got[2 * LEV : 3 * LEV, :]
        te[1, near] = got[3 * LEV : 4 * LEV, :]

    def unpack_pair(buf, i, landing):
        for side, rows in ((0, (0, 1)), (1, (4, 5))):
            for k, r in enumerate(rows):
                buf[i, r] = landing[side, k * LEV : (k + 1) * LEV, :]

    @pl.loop(0, 2)
    def _(i):
        adjoint_pair(i)
        put_masked()
        gather_adjoint()
        partner_wait(rsem, S0 + i, ev.at[i])
        gather_forward(ev.at[i])
        send_slots(i)

        @pl.when(i == 0)
        def _():
            for r in (2, 3):
                xa[r] = to[0, r] * adj[r]
            for r in (2, 3):
                u[1, r] = mix_row(xa, r, mtb)
            pack(back_s, [u[1, 2], u[1, 3]])
            beside_send(BACK, back_s, back_s, back_r)
            wait_bytes(rsem, DN, dn)
            nearby = jnp.concatenate([dn[0], dn[1]], axis=0)
            cells[:, 0:NT] = jnp.bitwise_and(nearby, 127)
            frow[NT // 2 :, :] = jnp.right_shift(nearby.T, 7) + jnp.where(first_half(NT), 8, 16)
            put_hot_columns(cells, BLOCKS // 2, BLOCKS)
            wait_bytes(rsem, FIRST, first_r)
            unpack_pair(f, 0, first_r)
            for side, near, far, inside in beyond:
                got = first_r.at[side]
                te[0, near] = got[2 * LEV : 3 * LEV, :]
                sp[far] = jnp.where(inside, got[3 * LEV : 4 * LEV, :], 0.0)
                for k in range(2):
                    st[4 * side + k] = got[4 * LEV + 2 * k : 4 * LEV + 2 * k + 2, :]
            wait_bytes(rsem, BACK, back_r)
            unpack_pair(u, 1, back_r)

        @pl.when(i == 1)
        def _():
            beside_send(NEXT, next_s, next_s, next_r)
            for k, ref in ((EDGE, edge_s), (FIRST, first_s), (BACK, back_r), (DN, dn)):
                wait_bytes(ssem, k, ref)
            partner_wait(ssem, S0, ev.at[0])
            partner_wait(ssem, S0 + 1, ev.at[1])
            partner_wait(ssem, TO, tro.at[0])
            sides_wait(ssem)
            wait_bytes(ssem, A0, rcv.at[0, :, 0 : NT - 1])
            wait_bytes(rsem, NEXT, next_r)
            unpack_pair(f, 1, next_r)

        wait_bytes(rsem, A0 + i, rcv.at[i, :, 0 : NT - 1])
        scatter_adjoint(i)
        @pl.when(i == 0)
        def _():
            each_partner(
                lambda p, d: [
                    remote(TS, ts.at[0, p], trs.at[1, me], (d, left)).start(),
                    remote(TS, ts.at[0, p], trs.at[0, me], (d, right)).start(),
                ]
            )

        each_partner(lambda p, d: remote(TO + i, ts.at[i, p], tro.at[i, me], (d, t)).start())
        scatter_forward(i)
        forward_pair(i)

        @pl.when(i == 0)
        def _():
            put_surface(1)
            surface_send(1)
            pack(next_s, [f[1, 2], f[1, 3]])
            partner_wait(rsem, TO, tro.at[0])
            sides_wait(rsem)
            for k, slots in enumerate((trs.at[0], tro.at[0], trs.at[1])):
                part = term_sum(slots)
                for e in range(2):
                    r = 2 * k + e
                    for c in range(3):
                        ls = slice(c * 128, (c + 1) * 128)
                        q = part[3 * e + c : 3 * e + c + 1, :] * st[r, 0:1, ls]
                        u[1, r, :, ls] = u[1, r, :, ls] + mtb[0] * q

    for r in (2, 3):
        out_ref[0, :, r - 2, :] = f[2, r]
        out_ref[1, :, r - 2, :] = adj[r]
    wait_bytes(ssem, NEXT, next_r)
    wait_bytes(ssem, A0 + 1, rcv.at[1, :, 0 : NT - 1])
    partner_wait(rsem, TO + 1, tro.at[1])
    part = term_sum(tro.at[1])
    for h in range(HI):
        ls = slice((h % 3) * 128, (h % 3 + 1) * 128)
        out_ref[1, 0, h // 3 : h // 3 + 1, ls] = adj[2 + h // 3, 0:1, ls] + part[h : h + 1, :]
    partner_wait(ssem, TO + 1, tro.at[1])


def per_device(
    initial, cotangent, spread_coef, trajectory, mixing, sea_mask, src_group, src_cell, weight, counts, dst_cell
):
    vmem = lambda *shape, dtype=F32: pltpu.VMEM(shape, dtype)
    field = vmem(6, LEV, COLS)
    operands = (
        initial[0], cotangent[0], spread_coef[0], trajectory[:, 0], jnp.transpose(mixing, (1, 0, 2)), sea_mask[0],
        src_group[0, 0].T, src_cell[0, 0].T, weight[0, 0].T, counts[0], dst_cell[0, 0].T,
    )
    (both,) = pl.pallas_call(
        kernel,
        out_shape=[jax.ShapeDtypeStruct((2, LEV, 2, COLS), F32)],
        in_specs=[pl.BlockSpec(memory_space=pltpu.HBM)] * 11,
        out_specs=[pl.BlockSpec(memory_space=pltpu.VMEM)],
        scratch_shapes=[pltpu.VMEM(a.shape, a.dtype) for a in operands]
        + [vmem(3, 6, LEV, COLS), vmem(2, 6, LEV, COLS), vmem(2, 6, LEV, COLS), vmem(2, 6, LEV, COLS)]
        + [field] * 6
        + [vmem(6, 2, COLS)]
        + [vmem(2, 48, COLS)] * 2
        + [vmem(2, 56, COLS)] * 2
        + [vmem(24, COLS), vmem(2, 24, COLS)] * 2
        + [vmem(2, CAP, NT, dtype=I32)]
        + [vmem(2, NATM + 1, 8, 128)]
        + [vmem(2, NATM, 8, 128)] * 3
        + [vmem(2, 2, NT, 1, 128)] * 2
        + [vmem(LEV, LEV)]
        + [vmem(LEV, LEV, 128)] * 2
        + [vmem(8, 128)] * 2
        + [vmem(NT, 128, dtype=I32)] * 3
        + [vmem(NT, 128), vmem(NT + 16, 128)]
        + [vmem(NT // 2, 128, dtype=I32)] * 2
        + [vmem(NT // 2, 128)] * 2
        + [vmem(128, 128, dtype=I32), vmem(3 * NT // 2, 128, dtype=I32)]
        + [vmem(3 * NT // 2, 128)]
        + [vmem(BLOCKS // 2, 128, 1024, dtype=BF16), vmem(3 * BLOCKS // 2, 1024, 128, dtype=BF16)]
        + [pltpu.SemaphoreType.DMA((12,))] * 2
        + [pltpu.SemaphoreType.DMA((11,))],
        compiler_params=pltpu.CompilerParams(
            collective_id=0, has_side_effects=True, vmem_limit_bytes=40 * 1024 * 1024
        ),
    )(*[pltpu.with_memory_space_constraint(a, pltpu.HBM) for a in operands])
    return both[0:1], both[1:2]


def solution(mesh):
    return jax.shard_map(
        per_device,
        mesh=mesh,
        in_specs=(
            P("comp", None, "tile", None),
            P("comp", None, "tile", None),
            P("comp", None, "tile", None),
            P(None, "comp", None, "tile", None),
            P("comp", None, None),
            P("comp", "tile", None),
            P("comp", "tile", None, None),
            P("comp", "tile", None, None),
            P("comp", "tile", None, None),
            P("comp", "tile", None),
            P("comp", "tile", None, None),
        ),
        out_specs=(P("comp", None, "tile", None), P("comp", None, "tile", None)),
        check_vma=False,
    )
```

```python
import functools

import jax
import jax.numpy as jnp
from jax import lax
from jax.experimental import pallas as pl
from jax.experimental.pallas import tpu as pltpu
from jax.sharding import PartitionSpec as P

MESH = pl.DeviceIdType.MESH
SPREAD = 0.12
NG, NATM, NT, LEV, COLS, CAP = 8, 6, 96, 12, 384, 64
NY, NZ = 8, 12
HI = 6
BLOCKS = NT // 8
RING_Y = (4, 3, 5, 2, 6, 1, 7)
RING_Z = (6, 5, 7, 4, 8, 3, 9, 2, 10, 1, 11)
F32, BF16, I32 = jnp.float32, jnp.bfloat16, jnp.int32

LOAD_ORDER = (4, 1, 3, 2, 0, 5, 9, 10, 7, 6, 8)
EDGE, FIRST, BACK, NEXT, DN, TS, S0, A0, TO = 0, 1, 2, 3, 4, 5, 6, 8, 10


def tile_offsets():
    offsets = [(a, b) for a in range(NY) for b in range(NZ) if (a, b) != (0, 0)]
    return sorted(offsets, key=lambda o: -(min(o[0], NY - o[0]) + min(o[1], NZ - o[1])))


def kernel(*refs):
    sources, out_ref, held, rest = refs[:11], refs[11], refs[12:23], refs[23:]
    init_ref, cot_ref, spread_ref, traj_ref, mix_ref, sea_ref, srcg_ref, srcc_ref, w_ref, cnt_ref, dst_ref = held
    (
        f, u, te, to, sp, wa, xa, ya, wb, adj, st,
        edge_s, edge_r, first_s, first_r, back_s, back_r, next_s, next_r, dn,
        ev, ts, tro, trs, snd, rcv,
        mat, mb, mtb, seat, mtab, gi, slo, shi, wv, val, plo, phi, pulled, alo, arow, aw, va, cells, frow, vf, hot_a, hot_f,
        ssem, rsem, isem, known,
    ) = rest
    g = lax.axis_index("comp")
    t = lax.axis_index("tile")
    y, z = t // NZ, lax.rem(t, NZ)
    right, left = lax.rem(t + 1, NT), lax.rem(t + NT - 1, NT)
    atmos = g < NATM
    ocean = g >= NATM
    me = jnp.where(atmos, g, g - NATM)

    def each_partner(act):
        @pl.when(atmos)
        def _():
            for p in range(NG - NATM):
                act(p, NATM + p)

        @pl.when(ocean)
        def _():
            for p in range(NATM):
                act(p, p)

    ys = [lax.rem(y + a, NY) * NZ for a in range(NY)]
    zs = [lax.rem(z + b, NZ) for b in range(NZ)]
    tiles = [ys[a] + zs[b] for a, b in tile_offsets()]

    def each_tile(act):
        for d in tiles:
            act(d)

    barrier = pltpu.get_barrier_semaphore()

    def greet(dev):
        pl.semaphore_signal(barrier, inc=1, device_id=dev, device_id_type=MESH)

    loads = [pltpu.make_async_copy(a, b, isem.at[n]) for n, (a, b) in enumerate(zip(sources, held))]
    for n in LOAD_ORDER:
        loads[n].start()
    for b in RING_Z:
        greet((g, ys[0] + zs[b]))
    column = [ys[a] + zs[0] for a in RING_Y]
    for d in column:
        greet((g, d))
    each_partner(lambda p, d: [greet((d, s)) for s in (left, right, t)])

    @pl.when(z == 0)
    def _():
        greet((g, left))

    @pl.when(z == NZ - 1)
    def _():
        greet((g, right))


    def remote(k, src, dst, dev):
        return pltpu.make_async_remote_copy(
            src_ref=src, dst_ref=dst, send_sem=ssem.at[k], recv_sem=rsem.at[k], device_id=dev, device_id_type=MESH
        )

    def beside_send(k, to_left, to_right, landing):
        remote(k, to_right, landing.at[0], (g, right)).start()
        remote(k, to_left, landing.at[1], (g, left)).start()

    def wait_bytes(sem, k, ref):
        pltpu.make_async_copy(ref, ref, sem.at[k]).wait()

    def partner_wait(sem, k, buf):
        @pl.when(atmos)
        def _():
            wait_bytes(sem, k, buf.at[0 : NG - NATM])

        @pl.when(ocean)
        def _():
            wait_bytes(sem, k, buf.at[0:NATM])

    def sides_wait(sem):
        slots = trs.reshape(1, 2 * NATM, 8, 128)

        @pl.when(atmos)
        def _():
            wait_bytes(sem, TS, slots.at[0, 0 : 2 * (NG - NATM)])

        @pl.when(ocean)
        def _():
            wait_bytes(sem, TS, slots.at[0])

    def surface_send(i):
        each_partner(lambda p, d: remote(S0 + i, ev.at[i, NATM], ev.at[i, me], (d, t)).start())

    lane = lax.broadcasted_iota(I32, (LEV, COLS), 1)

    def laplace(w, r):
        mid = w[r]
        west = jnp.where(lane == 0, 0.0, pltpu.roll(mid, 1, 1))
        east = jnp.where(lane == COLS - 1, 0.0, pltpu.roll(mid, COLS - 1, 1))
        return w[r + 1] + w[r - 1] + east + west - 4.0 * mid

    def mix_row(x, r, cols):
        parts = []
        for c in range(3):
            ls = slice(c * 128, (c + 1) * 128)
            acc = cols[0] * x[r, 0:1, ls]
            for m in range(1, LEV):
                acc = acc + cols[m] * x[r, m : m + 1, ls]
            parts.append(acc)
        return jnp.concatenate(parts, axis=1)

    def forward_pair(i):
        for r in range(6):
            wa[r] = sp[r] * f[i, r]
        for r in range(1, 5):
            xa[r] = f[i, r] + SPREAD * sp[r] * laplace(wa, r)
        for r in range(1, 5):
            row = te[i, r] * mix_row(xa, r, mb)
            ya[r] = row
            wb[r] = sp[r] * row
        for r in (2, 3):
            xa[r] = ya[r] + SPREAD * sp[r] * laplace(wb, r)
        for r in (2, 3):
            f[i + 1, r] = to[i, r] * mix_row(xa, r, mb)

    def adjoint_pair(i):
        for r in range(6):
            wa[r] = sp[r] * u[i, r]
        for r in range(1, 5):
            xa[r] = te[1 - i, r] * (u[i, r] + SPREAD * sp[r] * laplace(wa, r))
        for r in range(1, 5):
            row = mix_row(xa, r, mtb)
            ya[r] = row
            wb[r] = sp[r] * row
        for r in (2, 3):
            adj[r] = ya[r] + SPREAD * sp[r] * laplace(wb, r)

    def pack(dst, rows):
        at = 0
        for row in rows:
            dst[at : at + row.shape[0], :] = row
            at += row.shape[0]

    def surface_rows(strip):
        return [strip[r, 0:1, c * 128 : (c + 1) * 128] for r in (2, 3) for c in range(3)]

    def put_surface(i):
        for h, row in enumerate(surface_rows(f.at[i])):
            ev[i, NATM, h : h + 1, :] = row

    def put_masked():
        for h, row in enumerate(surface_rows(adj)):
            mtab[h : h + 1, :] = row * seat[h : h + 1, :]

    def first_half(rows):
        return lax.broadcasted_iota(I32, (rows, 128), 1) < CAP

    def pick(table, lo):
        return jnp.take_along_axis(table, lo, axis=1, mode="promise_in_bounds")

    def gather_adjoint():
        def body(i, carry):
            rows = pl.ds(pl.multiple_of(i * 8, 8), 8)
            lo, hi = plo[rows, :], phi[rows, :]
            out = jnp.zeros((8, 128), F32)
            for h in range(HI):
                table = jnp.broadcast_to(mtab[h : h + 1, :], (8, 128))
                out = jnp.where(hi == h, pick(table, lo), out)
            pulled[rows, :] = out
            return carry

        lax.fori_loop(0, BLOCKS // 2, body, 0, unroll=6)

    def gather_forward(owners):
        def body(i, carry):
            rows = pl.ds(pl.multiple_of(i * 8, 8), 8)
            lo, hi, owner = slo[rows, :], shi[rows, :], gi[rows, :]
            out = jnp.zeros((8, 128), F32)
            for h in range(HI):
                table = jnp.broadcast_to(owners[0, h : h + 1, :], (8, 128))
                for s in range(1, NATM):
                    table = jnp.where(owner == s, owners[s, h : h + 1, :], table)
                out = jnp.where(hi == h, pick(table, lo), out)
            val[pl.ds(pl.multiple_of(i * 8 + 8, 8), 8), :] = out * wv[rows, :]
            return carry

        lax.fori_loop(0, BLOCKS, body, 0, unroll=4)

    def put_beside(i):
        beside = snd.at[i, 1].reshape(NT, 128)
        beside[...] = jnp.where(first_half(NT), val[7 : 7 + NT, :], pltpu.roll(val[9 : 9 + NT, :], CAP, 1))

    def send_slots(i):
        own, mid = snd.at[i, 0].reshape(NT, 128), NT // 2
        own[0:mid] = jnp.where(first_half(mid), val[8 : 8 + mid, :], pltpu.roll(pulled[...], CAP, 1))
        own[mid:NT] = jnp.where(first_half(mid), val[8 + mid : 8 + NT, :], pulled[...])
        each_tile(lambda d: remote(A0 + i, snd.at[i, :, d], rcv.at[i, :, t], (g, d)).start())
        rcv[i, :, t] = snd[i, :, t]

    def packed(x):
        return jnp.where(first_half(NT // 2), x[0 : NT // 2], x[NT // 2 : NT])

    def scatter(value, index, hot, blocks, count, unroll, side):
        row_id = lax.broadcasted_iota(I32, (count, 128), 0)

        def body(i, acc):
            rows = pl.ds(pl.multiple_of(i * 8, 8), 8)
            v, where = value[rows, :], index[rows, :]
            top = v.astype(BF16).astype(F32)
            rest = v - top
            mid = rest.astype(BF16).astype(F32)
            low = rest - mid
            parts = []
            for j in range(8):
                hit = row_id == where[j : j + 1, :]
                parts.append(
                    jnp.concatenate([jnp.where(hit, p[j : j + 1, :], 0.0) for p in (top, mid, low)], axis=0).astype(BF16)
                )
            m = jnp.concatenate(parts, axis=1)
            return acc + lax.dot_general(m, hot[i], (((1,), (side,)), ((), ())), preferred_element_type=F32)

        acc = lax.fori_loop(0, blocks, body, jnp.zeros((3 * count, 128), F32), unroll=unroll)
        return acc[0:count] + acc[count : 2 * count] + acc[2 * count : 3 * count]

    def scatter_adjoint(i):
        got = rcv.at[i, 0].reshape(NT, 128)[...]
        va[...] = jnp.where(first_half(NT // 2), pltpu.roll(got[0 : NT // 2], CAP, 1), got[NT // 2 : NT]) * aw[...]
        total = scatter(va, arow, hot_a, BLOCKS // 2, 40, 6, 1)
        for p in range(NATM):
            ts[i, p, 0:HI, :] = total[p * HI : (p + 1) * HI, :]

    def scatter_forward(i):
        got = rcv.at[i, 0].reshape(NT, 128)[...]
        vf[0 : NT // 2, :] = jnp.where(first_half(NT // 2), got[0 : NT // 2], pltpu.roll(got[NT // 2 : NT], CAP, 1))
        vf[NT // 2 :, :] = rcv.at[i, 1].reshape(NT, 128)[...]
        total = scatter(vf, frow, hot_f, 3 * BLOCKS // 2, 24, 9, 0)
        for r in range(6):
            first = (8, 11, 0, 3, 16, 19)[r]
            for c in range(3):
                ls = slice(c * 128, (c + 1) * 128)
                f[i, r, 0:1, ls] = f[i, r, 0:1, ls] + total[first + c : first + c + 1, :] * st[r, 1:2, ls]

    def term_sum(slots):
        total = slots[0] + slots[1]
        for p in range(2, NATM):
            total = total + jnp.where(ocean, slots[p], 0.0)
        return total

    def put_hot(index, hot, start, stop):
        cell = lax.broadcasted_iota(I32, (128, 128), 0)

        @pl.loop(start, stop)
        def _(i):
            rows = index[pl.ds(pl.multiple_of(i * 8, 8), 8), :]
            for j in range(8):
                hit = jnp.where(cell == rows[j : j + 1, :], 1.0, 0.0).astype(BF16)
                hot[i, :, j * 128 : (j + 1) * 128] = hit

    def put_hot_columns(cells, first, start, count):
        target = lax.broadcasted_iota(I32, (128, 128), 1)

        @pl.loop(0, count)
        def _(i):
            columns = pltpu.roll(cells[...], lax.rem(128 - 8 * (first + i), 128), 1)
            for j in range(8):
                hit = jnp.where(target == columns[:, j : j + 1], 1.0, 0.0).astype(BF16)
                hot_f[start + i, j * 128 : (j + 1) * 128, :] = hit

    for n in LOAD_ORDER[:6]:
        loads[n].wait()
    diag = lax.broadcasted_iota(I32, (LEV, LEV), 0) == lax.broadcasted_iota(I32, (LEV, LEV), 1)
    for m in range(LEV):
        row = mix_ref[m]
        mat[m : m + 1, :] = row
        mtb[m] = jnp.broadcast_to(jnp.sum(jnp.where(diag, row, 0.0), axis=1, keepdims=True), (LEV, 128))
    for n in range(LEV):
        mb[n] = jnp.broadcast_to(mat[:, n : n + 1], (LEV, 128))
    for r in (0, 1):
        f[0, 2 + r] = init_ref[:, r, :]
        sp[2 + r] = spread_ref[:, r, :]
        te[0, 2 + r] = traj_ref[0, :, r, :]
        te[1, 2 + r] = traj_ref[2, :, r, :]
        to[0, 2 + r] = traj_ref[1, :, r, :]
        to[1, 2 + r] = traj_ref[3, :, r, :]
        xa[2 + r] = to[1, 2 + r] * cot_ref[:, r, :]
        st[2 + r, 0:1, :] = traj_ref[1, 0, r : r + 1, :]
        st[2 + r, 1:2, :] = sea_ref[r : r + 1, :].astype(F32)
    for r in (2, 3):
        u[0, r] = mix_row(xa, r, mtb)
    put_surface(0)
    for side, near in ((0, 2), (1, 3)):
        far = 5 - near
        pack(edge_s.at[side], [sp[near], u[0, near], sp[far] * u[0, far], te[1, near]])
        pack(first_s.at[side], [f[0, 2], f[0, 3], te[0, near], sp[far], st[2], st[3]])

    edge = jnp.where((z == 0) | (z == NZ - 1), 1, 0)
    pl.semaphore_wait(barrier, NY + NZ - 2 + edge + jnp.where(atmos, 3 * (NG - NATM), 3 * NATM))
    beside_send(EDGE, edge_s.at[0], edge_s.at[1], edge_r)
    for d in column:
        pl.semaphore_signal(known, inc=1, device_id=(g, d), device_id_type=MESH)
    surface_send(0)

    for n in LOAD_ORDER[6:]:
        loads[n].wait()
    for h in range(HI):
        seat[h : h + 1, :] = st[2 + h // 3, 1:2, (h % 3) * 128 : (h % 3 + 1) * 128]
    live = lax.broadcasted_iota(I32, (CAP, NT), 0) < cnt_ref[...]
    weight = jnp.where(live, w_ref[...], 0.0)
    wv[...] = jnp.concatenate([weight, weight], axis=0).T
    aw[...] = packed(wv[...])
    srcc, dstc = srcc_ref[...], dst_ref[...]
    srcg = srcg_ref[...] - jnp.where(atmos, NATM, 0)
    gi[...] = jnp.concatenate([srcg, srcg], axis=0).T
    send_cell = jnp.concatenate([srcc, srcc], axis=0).T
    slo[...] = jnp.bitwise_and(send_cell, 127)
    shi[...] = jnp.right_shift(send_cell, 7)
    alo[...] = packed(slo[...])
    arow[...] = HI * packed(gi[...]) + packed(shi[...])
    come = packed(jnp.concatenate([dstc, dstc], axis=0).T)
    plo[...] = jnp.bitwise_and(come, 127)
    phi[...] = jnp.right_shift(come, 7)
    frow[0 : NT // 2, :] = phi[...]
    val[0:8, :] = jnp.zeros((8, 128), F32)
    val[8 + NT : 16 + NT, :] = jnp.zeros((8, 128), F32)

    put_hot(alo, hot_a, 0, BLOCKS // 2)
    cells[0:CAP, 0 : NT // 2] = jnp.bitwise_and(dstc[:, 0 : NT // 2], 127)
    cells[CAP:, 0 : NT // 2] = jnp.bitwise_and(dstc[:, NT // 2 :], 127)
    put_hot_columns(cells, 0, 0, BLOCKS // 2)
    beside_send(DN, dst_ref, dst_ref, dn)

    partner_wait(rsem, S0, ev.at[0])
    gather_forward(ev.at[0])
    put_beside(0)
    wait_bytes(rsem, EDGE, edge_r)
    beyond = ((0, 1, 0, t > 0), (1, 4, 5, t < NT - 1))
    for side, near, far, inside in beyond:
        got = edge_r.at[side]
        sp[near] = jnp.where(inside, got[0:LEV, :], 0.0)
        u[0, near] = got[LEV : 2 * LEV, :]
        sp[far] = jnp.where(inside, jnp.ones((LEV, COLS), F32), 0.0)
        u[0, far] = got[2 * LEV : 3 * LEV, :]
        te[1, near] = got[3 * LEV : 4 * LEV, :]

    def unpack_pair(buf, i, landing):
        for side, rows in ((0, (0, 1)), (1, (4, 5))):
            for k, r in enumerate(rows):
                buf[i, r] = landing[side, k * LEV : (k + 1) * LEV, :]

    pl.semaphore_wait(known, NY - 1)
    @pl.loop(0, 2)
    def _(i):
        adjoint_pair(i)
        put_masked()
        gather_adjoint()
        @pl.when(i == 1)
        def _():
            partner_wait(rsem, S0 + 1, ev.at[1])
            gather_forward(ev.at[1])
            put_beside(1)

        send_slots(i)

        @pl.when(i == 0)
        def _():
            for r in (2, 3):
                xa[r] = to[0, r] * adj[r]
            for r in (2, 3):
                u[1, r] = mix_row(xa, r, mtb)
            pack(back_s, [u[1, 2], u[1, 3]])
            wait_bytes(rsem, DN, dn)
            nearby = jnp.concatenate([dn[0], dn[1]], axis=0)
            cells[:, 0:NT] = jnp.bitwise_and(nearby, 127)
            frow[NT // 2 :, :] = jnp.right_shift(nearby.T, 7) + jnp.where(first_half(NT), 8, 16)
            put_hot_columns(cells, 0, BLOCKS // 2, BLOCKS // 2)
            beside_send(FIRST, first_s.at[0], first_s.at[1], first_r)
            beside_send(BACK, back_s, back_s, back_r)
            put_hot_columns(cells, BLOCKS // 2, BLOCKS, BLOCKS // 2)

        @pl.when(i == 1)
        def _():
            beside_send(NEXT, next_s, next_s, next_r)
            for k, ref in ((EDGE, edge_s), (FIRST, first_s), (BACK, back_r), (DN, dn)):
                wait_bytes(ssem, k, ref)
            partner_wait(ssem, S0, ev.at[0])
            partner_wait(ssem, S0 + 1, ev.at[1])
            partner_wait(ssem, TO, tro.at[0])
            sides_wait(ssem)
            wait_bytes(ssem, A0, rcv.at[0, :, 0 : NT - 1])

        wait_bytes(rsem, A0 + i, rcv.at[i, :, 0 : NT - 1])
        scatter_adjoint(i)
        @pl.when(i == 0)
        def _():
            each_partner(
                lambda p, d: [
                    remote(TS, ts.at[0, p], trs.at[1, me], (d, left)).start(),
                    remote(TS, ts.at[0, p], trs.at[0, me], (d, right)).start(),
                ]
            )

        each_partner(lambda p, d: remote(TO + i, ts.at[i, p], tro.at[i, me], (d, t)).start())
        @pl.when(i == 0)
        def _():
            wait_bytes(rsem, FIRST, first_r)
            unpack_pair(f, 0, first_r)
            for side, near, far, inside in beyond:
                got = first_r.at[side]
                te[0, near] = got[2 * LEV : 3 * LEV, :]
                sp[far] = jnp.where(inside, got[3 * LEV : 4 * LEV, :], 0.0)
                for k in range(2):
                    st[4 * side + k] = got[4 * LEV + 2 * k : 4 * LEV + 2 * k + 2, :]

        @pl.when(i == 1)
        def _():
            wait_bytes(rsem, NEXT, next_r)
            unpack_pair(f, 1, next_r)

        scatter_forward(i)
        forward_pair(i)

        @pl.when(i == 0)
        def _():
            put_surface(1)
            surface_send(1)
            pack(next_s, [f[1, 2], f[1, 3]])
            wait_bytes(rsem, BACK, back_r)
            unpack_pair(u, 1, back_r)
            partner_wait(rsem, TO, tro.at[0])
            sides_wait(rsem)
            for k, slots in enumerate((trs.at[0], tro.at[0], trs.at[1])):
                part = term_sum(slots)
                for e in range(2):
                    r = 2 * k + e
                    for c in range(3):
                        ls = slice(c * 128, (c + 1) * 128)
                        q = part[3 * e + c : 3 * e + c + 1, :] * st[r, 0:1, ls]
                        u[1, r, :, ls] = u[1, r, :, ls] + mtb[0] * q

    for r in (2, 3):
        out_ref[0, :, r - 2, :] = f[2, r]
        out_ref[1, :, r - 2, :] = adj[r]
    wait_bytes(ssem, NEXT, next_r)
    wait_bytes(ssem, A0 + 1, rcv.at[1, :, 0 : NT - 1])
    partner_wait(rsem, TO + 1, tro.at[1])
    part = term_sum(tro.at[1])
    for h in range(HI):
        ls = slice((h % 3) * 128, (h % 3 + 1) * 128)
        out_ref[1, 0, h // 3 : h // 3 + 1, ls] = adj[2 + h // 3, 0:1, ls] + part[h : h + 1, :]
    partner_wait(ssem, TO + 1, tro.at[1])


def per_device(
    initial, cotangent, spread_coef, trajectory, mixing, sea_mask, src_group, src_cell, weight, counts, dst_cell
):
    vmem = lambda *shape, dtype=F32: pltpu.VMEM(shape, dtype)
    field = vmem(6, LEV, COLS)
    operands = (
        initial[0], cotangent[0], spread_coef[0], trajectory[:, 0], jnp.transpose(mixing, (1, 0, 2)), sea_mask[0],
        src_group[0, 0].T, src_cell[0, 0].T, weight[0, 0].T, counts[0], dst_cell[0, 0].T,
    )
    (both,) = pl.pallas_call(
        kernel,
        out_shape=[jax.ShapeDtypeStruct((2, LEV, 2, COLS), F32)],
        in_specs=[pl.BlockSpec(memory_space=pltpu.HBM)] * 11,
        out_specs=[pl.BlockSpec(memory_space=pltpu.VMEM)],
        scratch_shapes=[pltpu.VMEM(a.shape, a.dtype) for a in operands]
        + [vmem(3, 6, LEV, COLS), vmem(2, 6, LEV, COLS), vmem(2, 6, LEV, COLS), vmem(2, 6, LEV, COLS)]
        + [field] * 6
        + [vmem(6, 2, COLS)]
        + [vmem(2, 48, COLS)] * 2
        + [vmem(2, 56, COLS)] * 2
        + [vmem(24, COLS), vmem(2, 24, COLS)] * 2
        + [vmem(2, CAP, NT, dtype=I32)]
        + [vmem(2, NATM + 1, 8, 128)]
        + [vmem(2, NATM, 8, 128)] * 3
        + [vmem(2, 2, NT, 1, 128)] * 2
        + [vmem(LEV, LEV)]
        + [vmem(LEV, LEV, 128)] * 2
        + [vmem(8, 128)] * 2
        + [vmem(NT, 128, dtype=I32)] * 3
        + [vmem(NT, 128), vmem(NT + 16, 128)]
        + [vmem(NT // 2, 128, dtype=I32)] * 2
        + [vmem(NT // 2, 128)]
        + [vmem(NT // 2, 128, dtype=I32)] * 2
        + [vmem(NT // 2, 128)] * 2
        + [vmem(128, 128, dtype=I32), vmem(3 * NT // 2, 128, dtype=I32)]
        + [vmem(3 * NT // 2, 128)]
        + [vmem(BLOCKS // 2, 128, 1024, dtype=BF16), vmem(3 * BLOCKS // 2, 1024, 128, dtype=BF16)]
        + [pltpu.SemaphoreType.DMA((12,))] * 2
        + [pltpu.SemaphoreType.DMA((11,)), pltpu.SemaphoreType.REGULAR],
        compiler_params=pltpu.CompilerParams(
            collective_id=0, has_side_effects=True, vmem_limit_bytes=40 * 1024 * 1024
        ),
    )(*[pltpu.with_memory_space_constraint(a, pltpu.HBM) for a in operands])
    return both[0:1], both[1:2]


def solution(mesh):
    return jax.shard_map(
        per_device,
        mesh=mesh,
        in_specs=(
            P("comp", None, "tile", None),
            P("comp", None, "tile", None),
            P("comp", None, "tile", None),
            P(None, "comp", None, "tile", None),
            P("comp", None, None),
            P("comp", "tile", None),
            P("comp", "tile", None, None),
            P("comp", "tile", None, None),
            P("comp", "tile", None, None),
            P("comp", "tile", None),
            P("comp", "tile", None, None),
        ),
        out_specs=(P("comp", None, "tile", None), P("comp", None, "tile", None)),
        check_vma=False,
    )
```

```python
import functools

import jax
import jax.numpy as jnp
from jax import lax
from jax.experimental import pallas as pl
from jax.experimental.pallas import tpu as pltpu
from jax.sharding import PartitionSpec as P

MESH = pl.DeviceIdType.MESH
SPREAD = 0.12
NG, NATM, NT, LEV, COLS, CAP = 8, 6, 96, 12, 384, 64
NY, NZ = 8, 12
HI = 6
BLOCKS = NT // 8
RING_Y = (4, 3, 5, 2, 6, 1, 7)
NEAR_Z = (4, 8, 3, 9, 2, 10, 1, 11)
F32, BF16, I32 = jnp.float32, jnp.bfloat16, jnp.int32

LOAD_ORDER = (4, 1, 3, 2, 0, 5, 9, 10, 7, 6, 8)
EDGE, FIRST, BACK, NEXT, DN, TS, S0, A0, TO = 0, 1, 2, 3, 4, 5, 6, 8, 10


def tile_offsets():
    offsets = [(a, b) for a in range(NY) for b in range(NZ) if (a, b) != (0, 0)]
    return sorted(offsets, key=lambda o: -(min(o[0], NY - o[0]) + min(o[1], NZ - o[1])))


def kernel(*refs):
    sources, out_ref, held, rest = refs[:11], refs[11], refs[12:23], refs[23:]
    init_ref, cot_ref, spread_ref, traj_ref, mix_ref, sea_ref, srcg_ref, srcc_ref, w_ref, cnt_ref, dst_ref = held
    (
        f, u, te, to, sp, wa, xa, ya, wb, adj, st,
        edge_s, edge_r, first_s, first_r, back_s, back_r, next_s, next_r, dn,
        ev, ts, tro, trs, snd, rcv,
        mat, mb, mtb, seat, mtab, gi, slo, shi, wv, val, plo, phi, pulled, alo, arow, aw, va, cells, frow, vf, hot_a, hot_f,
        ssem, rsem, isem, known, known_row,
    ) = rest
    g = lax.axis_index("comp")
    t = lax.axis_index("tile")
    y, z = t // NZ, lax.rem(t, NZ)
    right, left = lax.rem(t + 1, NT), lax.rem(t + NT - 1, NT)
    atmos = g < NATM
    ocean = g >= NATM
    me = jnp.where(atmos, g, g - NATM)

    def each_partner(act):
        @pl.when(atmos)
        def _():
            for p in range(NG - NATM):
                act(p, NATM + p)

        @pl.when(ocean)
        def _():
            for p in range(NATM):
                act(p, p)

    ys = [lax.rem(y + a, NY) * NZ for a in range(NY)]
    zs = [lax.rem(z + b, NZ) for b in range(NZ)]
    tiles = [ys[a] + zs[b] for a, b in tile_offsets()]

    def each_tile(act):
        for d in tiles:
            act(d)

    barrier = pltpu.get_barrier_semaphore()

    def greet(dev):
        pl.semaphore_signal(barrier, inc=1, device_id=dev, device_id_type=MESH)

    loads = [pltpu.make_async_copy(a, b, isem.at[n]) for n, (a, b) in enumerate(zip(sources, held))]
    for n in LOAD_ORDER:
        loads[n].start()
    for b in NEAR_Z:
        greet((g, ys[0] + zs[b]))
    column = [ys[a] + zs[0] for a in RING_Y]
    for d in column:
        greet((g, d))
    each_partner(lambda p, d: [greet((d, s)) for s in (left, right, t)])

    @pl.when(z == 0)
    def _():
        greet((g, left))

    @pl.when(z == NZ - 1)
    def _():
        greet((g, right))


    def remote(k, src, dst, dev):
        return pltpu.make_async_remote_copy(
            src_ref=src, dst_ref=dst, send_sem=ssem.at[k], recv_sem=rsem.at[k], device_id=dev, device_id_type=MESH
        )

    def beside_send(k, to_left, to_right, landing):
        remote(k, to_right, landing.at[0], (g, right)).start()
        remote(k, to_left, landing.at[1], (g, left)).start()

    def wait_bytes(sem, k, ref):
        pltpu.make_async_copy(ref, ref, sem.at[k]).wait()

    def partner_wait(sem, k, buf):
        @pl.when(atmos)
        def _():
            wait_bytes(sem, k, buf.at[0 : NG - NATM])

        @pl.when(ocean)
        def _():
            wait_bytes(sem, k, buf.at[0:NATM])

    def sides_wait(sem):
        slots = trs.reshape(1, 2 * NATM, 8, 128)

        @pl.when(atmos)
        def _():
            wait_bytes(sem, TS, slots.at[0, 0 : 2 * (NG - NATM)])

        @pl.when(ocean)
        def _():
            wait_bytes(sem, TS, slots.at[0])

    def surface_send(i):
        each_partner(lambda p, d: remote(S0 + i, ev.at[i, NATM], ev.at[i, me], (d, t)).start())

    lane = lax.broadcasted_iota(I32, (LEV, COLS), 1)

    def laplace(w, r):
        mid = w[r]
        west = jnp.where(lane == 0, 0.0, pltpu.roll(mid, 1, 1))
        east = jnp.where(lane == COLS - 1, 0.0, pltpu.roll(mid, COLS - 1, 1))
        return w[r + 1] + w[r - 1] + east + west - 4.0 * mid

    def mix_row(x, r, cols):
        parts = []
        for c in range(3):
            ls = slice(c * 128, (c + 1) * 128)
            acc = cols[0] * x[r, 0:1, ls]
            for m in range(1, LEV):
                acc = acc + cols[m] * x[r, m : m + 1, ls]
            parts.append(acc)
        return jnp.concatenate(parts, axis=1)

    def forward_pair(i):
        for r in range(6):
            wa[r] = sp[r] * f[i, r]
        for r in range(1, 5):
            xa[r] = f[i, r] + SPREAD * sp[r] * laplace(wa, r)
        for r in range(1, 5):
            row = te[i, r] * mix_row(xa, r, mb)
            ya[r] = row
            wb[r] = sp[r] * row
        for r in (2, 3):
            xa[r] = ya[r] + SPREAD * sp[r] * laplace(wb, r)
        for r in (2, 3):
            f[i + 1, r] = to[i, r] * mix_row(xa, r, mb)

    def adjoint_pair(i):
        for r in range(6):
            wa[r] = sp[r] * u[i, r]
        for r in range(1, 5):
            xa[r] = te[1 - i, r] * (u[i, r] + SPREAD * sp[r] * laplace(wa, r))
        for r in range(1, 5):
            row = mix_row(xa, r, mtb)
            ya[r] = row
            wb[r] = sp[r] * row
        for r in (2, 3):
            adj[r] = ya[r] + SPREAD * sp[r] * laplace(wb, r)

    def pack(dst, rows):
        at = 0
        for row in rows:
            dst[at : at + row.shape[0], :] = row
            at += row.shape[0]

    def surface_rows(strip):
        return [strip[r, 0:1, c * 128 : (c + 1) * 128] for r in (2, 3) for c in range(3)]

    def put_surface(i):
        for h, row in enumerate(surface_rows(f.at[i])):
            ev[i, NATM, h : h + 1, :] = row

    def put_masked():
        for h, row in enumerate(surface_rows(adj)):
            mtab[h : h + 1, :] = row * seat[h : h + 1, :]

    def first_half(rows):
        return lax.broadcasted_iota(I32, (rows, 128), 1) < CAP

    def pick(table, lo):
        return jnp.take_along_axis(table, lo, axis=1, mode="promise_in_bounds")

    def gather_adjoint():
        def body(i, carry):
            rows = pl.ds(pl.multiple_of(i * 8, 8), 8)
            lo, hi = plo[rows, :], phi[rows, :]
            out = jnp.zeros((8, 128), F32)
            for h in range(HI):
                table = jnp.broadcast_to(mtab[h : h + 1, :], (8, 128))
                out = jnp.where(hi == h, pick(table, lo), out)
            pulled[rows, :] = out
            return carry

        lax.fori_loop(0, BLOCKS // 2, body, 0, unroll=6)

    def gather_forward(owners):
        def body(i, carry):
            rows = pl.ds(pl.multiple_of(i * 8, 8), 8)
            lo, hi, owner = slo[rows, :], shi[rows, :], gi[rows, :]
            out = jnp.zeros((8, 128), F32)
            for h in range(HI):
                table = jnp.broadcast_to(owners[0, h : h + 1, :], (8, 128))
                for s in range(1, NATM):
                    table = jnp.where(owner == s, owners[s, h : h + 1, :], table)
                out = jnp.where(hi == h, pick(table, lo), out)
            val[pl.ds(pl.multiple_of(i * 8 + 8, 8), 8), :] = out * wv[rows, :]
            return carry

        lax.fori_loop(0, BLOCKS, body, 0, unroll=6)

    def put_beside(i):
        beside = snd.at[i, 1].reshape(NT, 128)
        beside[...] = jnp.where(first_half(NT), val[7 : 7 + NT, :], pltpu.roll(val[9 : 9 + NT, :], CAP, 1))

    def send_slots(i):
        own, mid = snd.at[i, 0].reshape(NT, 128), NT // 2
        own[0:mid] = jnp.where(first_half(mid), val[8 : 8 + mid, :], pltpu.roll(pulled[...], CAP, 1))
        own[mid:NT] = jnp.where(first_half(mid), val[8 + mid : 8 + NT, :], pulled[...])
        each_tile(lambda d: remote(A0 + i, snd.at[i, :, d], rcv.at[i, :, t], (g, d)).start())
        rcv[i, :, t] = snd[i, :, t]

    def packed(x):
        return jnp.where(first_half(NT // 2), x[0 : NT // 2], x[NT // 2 : NT])

    def scatter(value, index, hot, blocks, count, unroll, side):
        row_id = lax.broadcasted_iota(I32, (count, 128), 0)

        def body(i, acc):
            rows = pl.ds(pl.multiple_of(i * 8, 8), 8)
            v, where = value[rows, :], index[rows, :]
            top = v.astype(BF16).astype(F32)
            rest = v - top
            mid = rest.astype(BF16).astype(F32)
            low = rest - mid
            parts = []
            for j in range(8):
                hit = row_id == where[j : j + 1, :]
                parts.append(
                    jnp.concatenate([jnp.where(hit, p[j : j + 1, :], 0.0) for p in (top, mid, low)], axis=0).astype(BF16)
                )
            m = jnp.concatenate(parts, axis=1)
            return acc + lax.dot_general(m, hot[i], (((1,), (side,)), ((), ())), preferred_element_type=F32)

        acc = lax.fori_loop(0, blocks, body, jnp.zeros((3 * count, 128), F32), unroll=unroll)
        return acc[0:count] + acc[count : 2 * count] + acc[2 * count : 3 * count]

    def scatter_adjoint(i):
        got = rcv.at[i, 0].reshape(NT, 128)[...]
        va[...] = jnp.where(first_half(NT // 2), pltpu.roll(got[0 : NT // 2], CAP, 1), got[NT // 2 : NT]) * aw[...]
        total = scatter(va, arow, hot_a, BLOCKS // 2, 40, 6, 1)
        for p in range(NATM):
            ts[i, p, 0:HI, :] = total[p * HI : (p + 1) * HI, :]

    def scatter_forward(i):
        got = rcv.at[i, 0].reshape(NT, 128)[...]
        vf[0 : NT // 2, :] = jnp.where(first_half(NT // 2), got[0 : NT // 2], pltpu.roll(got[NT // 2 : NT], CAP, 1))
        vf[NT // 2 :, :] = rcv.at[i, 1].reshape(NT, 128)[...]
        total = scatter(vf, frow, hot_f, 3 * BLOCKS // 2, 24, 9, 0)
        for r in range(6):
            first = (8, 11, 0, 3, 16, 19)[r]
            for c in range(3):
                ls = slice(c * 128, (c + 1) * 128)
                f[i, r, 0:1, ls] = f[i, r, 0:1, ls] + total[first + c : first + c + 1, :] * st[r, 1:2, ls]

    def term_sum(slots):
        total = slots[0] + slots[1]
        for p in range(2, NATM):
            total = total + jnp.where(ocean, slots[p], 0.0)
        return total

    def put_hot(index, hot, start, stop):
        cell = lax.broadcasted_iota(I32, (128, 128), 0)

        @pl.loop(start, stop)
        def _(i):
            rows = index[pl.ds(pl.multiple_of(i * 8, 8), 8), :]
            for j in range(8):
                hit = jnp.where(cell == rows[j : j + 1, :], 1.0, 0.0).astype(BF16)
                hot[i, :, j * 128 : (j + 1) * 128] = hit

    def put_hot_columns(cells, first, start, count):
        target = lax.broadcasted_iota(I32, (128, 128), 1)

        @pl.loop(0, count)
        def _(i):
            columns = pltpu.roll(cells[...], lax.rem(128 - 8 * (first + i), 128), 1)
            for j in range(8):
                hit = jnp.where(target == columns[:, j : j + 1], 1.0, 0.0).astype(BF16)
                hot_f[start + i, j * 128 : (j + 1) * 128, :] = hit

    for n in LOAD_ORDER[:6]:
        loads[n].wait()
    diag = lax.broadcasted_iota(I32, (LEV, LEV), 0) == lax.broadcasted_iota(I32, (LEV, LEV), 1)
    for m in range(LEV):
        row = mix_ref[m]
        mat[m : m + 1, :] = row
        mtb[m] = jnp.broadcast_to(jnp.sum(jnp.where(diag, row, 0.0), axis=1, keepdims=True), (LEV, 128))
    for n in range(LEV):
        mb[n] = jnp.broadcast_to(mat[:, n : n + 1], (LEV, 128))
    for r in (0, 1):
        f[0, 2 + r] = init_ref[:, r, :]
        sp[2 + r] = spread_ref[:, r, :]
        te[0, 2 + r] = traj_ref[0, :, r, :]
        te[1, 2 + r] = traj_ref[2, :, r, :]
        to[0, 2 + r] = traj_ref[1, :, r, :]
        to[1, 2 + r] = traj_ref[3, :, r, :]
        xa[2 + r] = to[1, 2 + r] * cot_ref[:, r, :]
        st[2 + r, 0:1, :] = traj_ref[1, 0, r : r + 1, :]
        st[2 + r, 1:2, :] = sea_ref[r : r + 1, :].astype(F32)
    for r in (2, 3):
        u[0, r] = mix_row(xa, r, mtb)
    put_surface(0)
    for side, near in ((0, 2), (1, 3)):
        far = 5 - near
        pack(edge_s.at[side], [sp[near], u[0, near], sp[far] * u[0, far], te[1, near]])
        pack(first_s.at[side], [f[0, 2], f[0, 3], te[0, near], sp[far], st[2], st[3]])

    edge = jnp.where((z == 0) | (z == NZ - 1), 1, 0)
    pl.semaphore_wait(barrier, NY - 1 + len(NEAR_Z) + edge + jnp.where(atmos, 3 * (NG - NATM), 3 * NATM))
    beside_send(EDGE, edge_s.at[0], edge_s.at[1], edge_r)
    for d in column:
        pl.semaphore_signal(known, inc=1, device_id=(g, d), device_id_type=MESH)
    surface_send(0)

    for n in LOAD_ORDER[6:]:
        loads[n].wait()
    for h in range(HI):
        seat[h : h + 1, :] = st[2 + h // 3, 1:2, (h % 3) * 128 : (h % 3 + 1) * 128]
    live = lax.broadcasted_iota(I32, (CAP, NT), 0) < cnt_ref[...]
    weight = jnp.where(live, w_ref[...], 0.0)
    wv[...] = jnp.concatenate([weight, weight], axis=0).T
    aw[...] = packed(wv[...])
    srcc, dstc = srcc_ref[...], dst_ref[...]
    srcg = srcg_ref[...] - jnp.where(atmos, NATM, 0)
    gi[...] = jnp.concatenate([srcg, srcg], axis=0).T
    send_cell = jnp.concatenate([srcc, srcc], axis=0).T
    slo[...] = jnp.bitwise_and(send_cell, 127)
    shi[...] = jnp.right_shift(send_cell, 7)
    alo[...] = packed(slo[...])
    arow[...] = HI * packed(gi[...]) + packed(shi[...])
    come = packed(jnp.concatenate([dstc, dstc], axis=0).T)
    plo[...] = jnp.bitwise_and(come, 127)
    phi[...] = jnp.right_shift(come, 7)
    frow[0 : NT // 2, :] = phi[...]
    val[0:8, :] = jnp.zeros((8, 128), F32)
    val[8 + NT : 16 + NT, :] = jnp.zeros((8, 128), F32)

    put_hot(alo, hot_a, 0, BLOCKS // 2)
    cells[0:CAP, 0 : NT // 2] = jnp.bitwise_and(dstc[:, 0 : NT // 2], 127)
    cells[CAP:, 0 : NT // 2] = jnp.bitwise_and(dstc[:, NT // 2 :], 127)
    put_hot_columns(cells, 0, 0, BLOCKS // 2)
    beside_send(DN, dst_ref, dst_ref, dn)

    pl.semaphore_wait(known, NY - 1)
    for b in (2, NZ - 2):
        pl.semaphore_signal(known_row, inc=1, device_id=(g, ys[0] + zs[b]), device_id_type=MESH)
    partner_wait(rsem, S0, ev.at[0])
    gather_forward(ev.at[0])
    put_beside(0)
    wait_bytes(rsem, EDGE, edge_r)
    beyond = ((0, 1, 0, t > 0), (1, 4, 5, t < NT - 1))
    for side, near, far, inside in beyond:
        got = edge_r.at[side]
        sp[near] = jnp.where(inside, got[0:LEV, :], 0.0)
        u[0, near] = got[LEV : 2 * LEV, :]
        sp[far] = jnp.where(inside, jnp.ones((LEV, COLS), F32), 0.0)
        u[0, far] = got[2 * LEV : 3 * LEV, :]
        te[1, near] = got[3 * LEV : 4 * LEV, :]

    def unpack_pair(buf, i, landing):
        for side, rows in ((0, (0, 1)), (1, (4, 5))):
            for k, r in enumerate(rows):
                buf[i, r] = landing[side, k * LEV : (k + 1) * LEV, :]

    @pl.loop(0, 2)
    def _(i):
        adjoint_pair(i)
        put_masked()
        gather_adjoint()
        @pl.when(i == 1)
        def _():
            partner_wait(rsem, S0 + 1, ev.at[1])
            gather_forward(ev.at[1])
            put_beside(1)

        @pl.when(i == 0)
        def _():
            pl.semaphore_wait(known_row, 2)

        send_slots(i)

        @pl.when(i == 0)
        def _():
            for r in (2, 3):
                xa[r] = to[0, r] * adj[r]
            for r in (2, 3):
                u[1, r] = mix_row(xa, r, mtb)
            pack(back_s, [u[1, 2], u[1, 3]])
            wait_bytes(rsem, DN, dn)
            nearby = jnp.concatenate([dn[0], dn[1]], axis=0)
            cells[:, 0:NT] = jnp.bitwise_and(nearby, 127)
            frow[NT // 2 :, :] = jnp.right_shift(nearby.T, 7) + jnp.where(first_half(NT), 8, 16)
            put_hot_columns(cells, 0, BLOCKS // 2, BLOCKS // 2)
            beside_send(FIRST, first_s.at[0], first_s.at[1], first_r)
            beside_send(BACK, back_s, back_s, back_r)
            put_hot_columns(cells, BLOCKS // 2, BLOCKS, BLOCKS // 2)

        @pl.when(i == 1)
        def _():
            beside_send(NEXT, next_s, next_s, next_r)
            for k, ref in ((EDGE, edge_s), (FIRST, first_s), (BACK, back_r), (DN, dn)):
                wait_bytes(ssem, k, ref)
            partner_wait(ssem, S0, ev.at[0])
            partner_wait(ssem, S0 + 1, ev.at[1])
            partner_wait(ssem, TO, tro.at[0])
            sides_wait(ssem)
            wait_bytes(ssem, A0, rcv.at[0, :, 0 : NT - 1])

        wait_bytes(rsem, A0 + i, rcv.at[i, :, 0 : NT - 1])
        scatter_adjoint(i)
        @pl.when(i == 0)
        def _():
            each_partner(
                lambda p, d: [
                    remote(TS, ts.at[0, p], trs.at[1, me], (d, left)).start(),
                    remote(TS, ts.at[0, p], trs.at[0, me], (d, right)).start(),
                ]
            )

        each_partner(lambda p, d: remote(TO + i, ts.at[i, p], tro.at[i, me], (d, t)).start())
        @pl.when(i == 0)
        def _():
            wait_bytes(rsem, FIRST, first_r)
            unpack_pair(f, 0, first_r)
            for side, near, far, inside in beyond:
                got = first_r.at[side]
                te[0, near] = got[2 * LEV : 3 * LEV, :]
                sp[far] = jnp.where(inside, got[3 * LEV : 4 * LEV, :], 0.0)
                for k in range(2):
                    st[4 * side + k] = got[4 * LEV + 2 * k : 4 * LEV + 2 * k + 2, :]

        @pl.when(i == 1)
        def _():
            wait_bytes(rsem, NEXT, next_r)
            unpack_pair(f, 1, next_r)

        scatter_forward(i)
        forward_pair(i)

        @pl.when(i == 0)
        def _():
            put_surface(1)
            surface_send(1)
            pack(next_s, [f[1, 2], f[1, 3]])
            wait_bytes(rsem, BACK, back_r)
            unpack_pair(u, 1, back_r)
            partner_wait(rsem, TO, tro.at[0])
            sides_wait(rsem)
            for k, slots in enumerate((trs.at[0], tro.at[0], trs.at[1])):
                part = term_sum(slots)
                for e in range(2):
                    r = 2 * k + e
                    for c in range(3):
                        ls = slice(c * 128, (c + 1) * 128)
                        q = part[3 * e + c : 3 * e + c + 1, :] * st[r, 0:1, ls]
                        u[1, r, :, ls] = u[1, r, :, ls] + mtb[0] * q

    for r in (2, 3):
        out_ref[0, :, r - 2, :] = f[2, r]
        out_ref[1, :, r - 2, :] = adj[r]
    wait_bytes(ssem, NEXT, next_r)
    wait_bytes(ssem, A0 + 1, rcv.at[1, :, 0 : NT - 1])
    partner_wait(rsem, TO + 1, tro.at[1])
    part = term_sum(tro.at[1])
    for h in range(HI):
        ls = slice((h % 3) * 128, (h % 3 + 1) * 128)
        out_ref[1, 0, h // 3 : h // 3 + 1, ls] = adj[2 + h // 3, 0:1, ls] + part[h : h + 1, :]
    partner_wait(ssem, TO + 1, tro.at[1])


def per_device(
    initial, cotangent, spread_coef, trajectory, mixing, sea_mask, src_group, src_cell, weight, counts, dst_cell
):
    vmem = lambda *shape, dtype=F32: pltpu.VMEM(shape, dtype)
    field = vmem(6, LEV, COLS)
    operands = (
        initial[0], cotangent[0], spread_coef[0], trajectory[:, 0], jnp.transpose(mixing, (1, 0, 2)), sea_mask[0],
        src_group[0, 0].T, src_cell[0, 0].T, weight[0, 0].T, counts[0], dst_cell[0, 0].T,
    )
    (both,) = pl.pallas_call(
        kernel,
        out_shape=[jax.ShapeDtypeStruct((2, LEV, 2, COLS), F32)],
        in_specs=[pl.BlockSpec(memory_space=pltpu.HBM)] * 11,
        out_specs=[pl.BlockSpec(memory_space=pltpu.VMEM)],
        scratch_shapes=[pltpu.VMEM(a.shape, a.dtype) for a in operands]
        + [vmem(3, 6, LEV, COLS), vmem(2, 6, LEV, COLS), vmem(2, 6, LEV, COLS), vmem(2, 6, LEV, COLS)]
        + [field] * 6
        + [vmem(6, 2, COLS)]
        + [vmem(2, 48, COLS)] * 2
        + [vmem(2, 56, COLS)] * 2
        + [vmem(24, COLS), vmem(2, 24, COLS)] * 2
        + [vmem(2, CAP, NT, dtype=I32)]
        + [vmem(2, NATM + 1, 8, 128)]
        + [vmem(2, NATM, 8, 128)] * 3
        + [vmem(2, 2, NT, 1, 128)] * 2
        + [vmem(LEV, LEV)]
        + [vmem(LEV, LEV, 128)] * 2
        + [vmem(8, 128)] * 2
        + [vmem(NT, 128, dtype=I32)] * 3
        + [vmem(NT, 128), vmem(NT + 16, 128)]
        + [vmem(NT // 2, 128, dtype=I32)] * 2
        + [vmem(NT // 2, 128)]
        + [vmem(NT // 2, 128, dtype=I32)] * 2
        + [vmem(NT // 2, 128)] * 2
        + [vmem(128, 128, dtype=I32), vmem(3 * NT // 2, 128, dtype=I32)]
        + [vmem(3 * NT // 2, 128)]
        + [vmem(BLOCKS // 2, 128, 1024, dtype=BF16), vmem(3 * BLOCKS // 2, 1024, 128, dtype=BF16)]
        + [pltpu.SemaphoreType.DMA((12,))] * 2
        + [pltpu.SemaphoreType.DMA((11,)), pltpu.SemaphoreType.REGULAR, pltpu.SemaphoreType.REGULAR],
        compiler_params=pltpu.CompilerParams(
            collective_id=0, has_side_effects=True, vmem_limit_bytes=40 * 1024 * 1024
        ),
    )(*[pltpu.with_memory_space_constraint(a, pltpu.HBM) for a in operands])
    return both[0:1], both[1:2]


def solution(mesh):
    return jax.shard_map(
        per_device,
        mesh=mesh,
        in_specs=(
            P("comp", None, "tile", None),
            P("comp", None, "tile", None),
            P("comp", None, "tile", None),
            P(None, "comp", None, "tile", None),
            P("comp", None, None),
            P("comp", "tile", None),
            P("comp", "tile", None, None),
            P("comp", "tile", None, None),
            P("comp", "tile", None, None),
            P("comp", "tile", None),
            P("comp", "tile", None, None),
        ),
        out_specs=(P("comp", None, "tile", None), P("comp", None, "tile", None)),
        check_vma=False,
    )
```

```python
import functools

import jax
import jax.numpy as jnp
from jax import lax
from jax.experimental import pallas as pl
from jax.experimental.pallas import tpu as pltpu
from jax.sharding import PartitionSpec as P

MESH = pl.DeviceIdType.MESH
SPREAD = 0.12
NG, NATM, NT, LEV, COLS, CAP = 8, 6, 96, 12, 384, 64
NY, NZ = 8, 12
HI = 6
BLOCKS = NT // 8
RING_Y = (4, 3, 5, 2, 6, 1, 7)
NEAR_Z = (4, 8, 3, 9, 2, 10, 1, 11)
F32, BF16, I32 = jnp.float32, jnp.bfloat16, jnp.int32

LOAD_ORDER = (4, 1, 3, 2, 0, 5, 9, 10, 7, 6, 8)
EDGE, FIRST, BACK, NEXT, DN, TS, S0, A0, TO, REST = 0, 1, 2, 3, 4, 5, 6, 8, 10, 12


def tile_offsets():
    offsets = [(a, b) for a in range(NY) for b in range(NZ) if (a, b) != (0, 0)]
    return sorted(offsets, key=lambda o: -(min(o[0], NY - o[0]) + min(o[1], NZ - o[1])))


def kernel(*refs):
    sources, out_ref, held, rest = refs[:11], refs[11], refs[12:23], refs[23:]
    init_ref, cot_ref, spread_ref, traj_ref, mix_ref, sea_ref, srcg_ref, srcc_ref, w_ref, cnt_ref, dst_ref = held
    (
        f, u, te, to, sp, wa, xa, ya, wb, adj, st,
        edge_s, edge_r, rest_s, rest_r, first_s, first_r, back_s, back_r, next_s, next_r, dn,
        ev, ts, tro, trs, snd, rcv,
        mat, mb, mtb, seat, mtab, gi, slo, shi, wv, val, plo, phi, pulled, alo, arow, aw, va, cells, frow, vf, hot_a, hot_f,
        ssem, rsem, isem, known, known_row,
    ) = rest
    g = lax.axis_index("comp")
    t = lax.axis_index("tile")
    y, z = t // NZ, lax.rem(t, NZ)
    right, left = lax.rem(t + 1, NT), lax.rem(t + NT - 1, NT)
    atmos = g < NATM
    ocean = g >= NATM
    me = jnp.where(atmos, g, g - NATM)

    def each_partner(act):
        @pl.when(atmos)
        def _():
            for p in range(NG - NATM):
                act(p, NATM + p)

        @pl.when(ocean)
        def _():
            for p in range(NATM):
                act(p, p)

    ys = [lax.rem(y + a, NY) * NZ for a in range(NY)]
    zs = [lax.rem(z + b, NZ) for b in range(NZ)]
    tiles = [ys[a] + zs[b] for a, b in tile_offsets()]

    def each_tile(act):
        for d in tiles:
            act(d)

    barrier = pltpu.get_barrier_semaphore()

    def greet(dev):
        pl.semaphore_signal(barrier, inc=1, device_id=dev, device_id_type=MESH)

    loads = [pltpu.make_async_copy(a, b, isem.at[n]) for n, (a, b) in enumerate(zip(sources, held))]
    for n in LOAD_ORDER:
        loads[n].start()
    for b in NEAR_Z:
        greet((g, ys[0] + zs[b]))
    column = [ys[a] + zs[0] for a in RING_Y]
    for d in column:
        greet((g, d))
    each_partner(lambda p, d: [greet((d, s)) for s in (left, right, t)])

    @pl.when(z == 0)
    def _():
        greet((g, left))

    @pl.when(z == NZ - 1)
    def _():
        greet((g, right))


    def remote(k, src, dst, dev):
        return pltpu.make_async_remote_copy(
            src_ref=src, dst_ref=dst, send_sem=ssem.at[k], recv_sem=rsem.at[k], device_id=dev, device_id_type=MESH
        )

    def beside_send(k, to_left, to_right, landing):
        remote(k, to_right, landing.at[0], (g, right)).start()
        remote(k, to_left, landing.at[1], (g, left)).start()

    def wait_bytes(sem, k, ref):
        pltpu.make_async_copy(ref, ref, sem.at[k]).wait()

    def partner_wait(sem, k, buf):
        @pl.when(atmos)
        def _():
            wait_bytes(sem, k, buf.at[0 : NG - NATM])

        @pl.when(ocean)
        def _():
            wait_bytes(sem, k, buf.at[0:NATM])

    def sides_wait(sem):
        slots = trs.reshape(1, 2 * NATM, 8, 128)

        @pl.when(atmos)
        def _():
            wait_bytes(sem, TS, slots.at[0, 0 : 2 * (NG - NATM)])

        @pl.when(ocean)
        def _():
            wait_bytes(sem, TS, slots.at[0])

    def surface_send(i):
        each_partner(lambda p, d: remote(S0 + i, ev.at[i, NATM], ev.at[i, me], (d, t)).start())

    def sideways(mid):
        column = lax.broadcasted_iota(I32, mid.shape, 1)
        west = jnp.where(column == 0, 0.0, pltpu.roll(mid, 1, 1))
        east = jnp.where(column == COLS - 1, 0.0, pltpu.roll(mid, COLS - 1, 1))
        return east + west

    def laplace(w, r):
        mid = w[r]
        return w[r + 1] + w[r - 1] + sideways(mid) - 4.0 * mid

    def level_zero(x):
        weights = jnp.concatenate([mb[0]] * 3, axis=1)
        return jnp.sum(weights * x, axis=0, keepdims=True)

    def mix_row(x, r, cols):
        parts = []
        for c in range(3):
            ls = slice(c * 128, (c + 1) * 128)
            acc = cols[0] * x[r, 0:1, ls]
            for m in range(1, LEV):
                acc = acc + cols[m] * x[r, m : m + 1, ls]
            parts.append(acc)
        return jnp.concatenate(parts, axis=1)

    def forward_pair(i):
        for r in range(6):
            wa[r] = sp[r] * f[i, r]
        for r in range(1, 5):
            xa[r] = f[i, r] + SPREAD * sp[r] * laplace(wa, r)
        for r in range(1, 5):
            row = te[i, r] * mix_row(xa, r, mb)
            ya[r] = row
            wb[r] = sp[r] * row
        for r in (2, 3):
            xa[r] = ya[r] + SPREAD * sp[r] * laplace(wb, r)
        for r in (2, 3):
            f[i + 1, r] = to[i, r] * mix_row(xa, r, mb)

    def adjoint_pair(i):
        for r in range(6):
            wa[r] = sp[r] * u[i, r]
        for r in range(1, 5):
            xa[r] = te[1 - i, r] * (u[i, r] + SPREAD * sp[r] * laplace(wa, r))
        second_step()

    def second_step():
        for r in range(1, 5):
            row = mix_row(xa, r, mtb)
            ya[r] = row
            wb[r] = sp[r] * row
        for r in (2, 3):
            adj[r] = ya[r] + SPREAD * sp[r] * laplace(wb, r)

    def first_surface():
        for r in (2, 3):
            xa[r] = te[1, r] * (u[0, r] + SPREAD * sp[r] * laplace(wa, r))
        tops = {r: level_zero(xa[r]) for r in (2, 3)}
        coef = {r: sp[r, 0:1, :] for r in (2, 3)}
        for side, near, far, inside in beyond:
            inner = 2 + side
            got = edge_r.at[side]
            xa[near] = got[LEV : 2 * LEV, :] * wa[inner]
            tops[near] = got[2 * LEV : 2 * LEV + 1, :] + level_zero(xa[near])
            coef[near] = jnp.where(inside, got[2 * LEV + 1 : 2 * LEV + 2, :], 0.0)
        scaled = {r: coef[r] * tops[r] for r in range(1, 5)}
        for r in (2, 3):
            around = scaled[r + 1] + scaled[r - 1] + sideways(scaled[r]) - 4.0 * scaled[r]
            adj[r, 0:1, :] = tops[r] + SPREAD * coef[r] * around

    def pack(dst, rows):
        at = 0
        for row in rows:
            dst[at : at + row.shape[0], :] = row
            at += row.shape[0]

    def surface_rows(strip):
        return [strip[r, 0:1, c * 128 : (c + 1) * 128] for r in (2, 3) for c in range(3)]

    def put_surface(i):
        for h, row in enumerate(surface_rows(f.at[i])):
            ev[i, NATM, h : h + 1, :] = row

    def put_masked():
        for h, row in enumerate(surface_rows(adj)):
            mtab[h : h + 1, :] = row * seat[h : h + 1, :]

    def first_half(rows):
        return lax.broadcasted_iota(I32, (rows, 128), 1) < CAP

    def pick(table, lo):
        return jnp.take_along_axis(table, lo, axis=1, mode="promise_in_bounds")

    def gather_adjoint():
        def body(i, carry):
            rows = pl.ds(pl.multiple_of(i * 8, 8), 8)
            lo, hi = plo[rows, :], phi[rows, :]
            out = jnp.zeros((8, 128), F32)
            for h in range(HI):
                table = jnp.broadcast_to(mtab[h : h + 1, :], (8, 128))
                out = jnp.where(hi == h, pick(table, lo), out)
            pulled[rows, :] = out
            return carry

        lax.fori_loop(0, BLOCKS // 2, body, 0, unroll=6)

    def gather_forward(owners):
        def body(i, carry):
            rows = pl.ds(pl.multiple_of(i * 8, 8), 8)
            lo, hi, owner = slo[rows, :], shi[rows, :], gi[rows, :]
            out = jnp.zeros((8, 128), F32)
            for h in range(HI):
                table = jnp.broadcast_to(owners[0, h : h + 1, :], (8, 128))
                for s in range(1, NATM):
                    table = jnp.where(owner == s, owners[s, h : h + 1, :], table)
                out = jnp.where(hi == h, pick(table, lo), out)
            val[pl.ds(pl.multiple_of(i * 8 + 8, 8), 8), :] = out * wv[rows, :]
            return carry

        lax.fori_loop(0, BLOCKS, body, 0, unroll=6)

    def put_beside(i):
        beside = snd.at[i, 1].reshape(NT, 128)
        beside[...] = jnp.where(first_half(NT), val[7 : 7 + NT, :], pltpu.roll(val[9 : 9 + NT, :], CAP, 1))

    def send_slots(i):
        own, mid = snd.at[i, 0].reshape(NT, 128), NT // 2
        own[0:mid] = jnp.where(first_half(mid), val[8 : 8 + mid, :], pltpu.roll(pulled[...], CAP, 1))
        own[mid:NT] = jnp.where(first_half(mid), val[8 + mid : 8 + NT, :], pulled[...])
        each_tile(lambda d: remote(A0 + i, snd.at[i, :, d], rcv.at[i, :, t], (g, d)).start())
        rcv[i, :, t] = snd[i, :, t]

    def packed(x):
        return jnp.where(first_half(NT // 2), x[0 : NT // 2], x[NT // 2 : NT])

    def scatter(value, index, hot, blocks, count, unroll, side):
        row_id = lax.broadcasted_iota(I32, (count, 128), 0)

        def body(i, acc):
            rows = pl.ds(pl.multiple_of(i * 8, 8), 8)
            v, where = value[rows, :], index[rows, :]
            top = v.astype(BF16).astype(F32)
            rest = v - top
            mid = rest.astype(BF16).astype(F32)
            low = rest - mid
            parts = []
            for j in range(8):
                hit = row_id == where[j : j + 1, :]
                parts.append(
                    jnp.concatenate([jnp.where(hit, p[j : j + 1, :], 0.0) for p in (top, mid, low)], axis=0).astype(BF16)
                )
            m = jnp.concatenate(parts, axis=1)
            return acc + lax.dot_general(m, hot[i], (((1,), (side,)), ((), ())), preferred_element_type=F32)

        acc = lax.fori_loop(0, blocks, body, jnp.zeros((3 * count, 128), F32), unroll=unroll)
        return acc[0:count] + acc[count : 2 * count] + acc[2 * count : 3 * count]

    def scatter_adjoint(i):
        got = rcv.at[i, 0].reshape(NT, 128)[...]
        va[...] = jnp.where(first_half(NT // 2), pltpu.roll(got[0 : NT // 2], CAP, 1), got[NT // 2 : NT]) * aw[...]
        total = scatter(va, arow, hot_a, BLOCKS // 2, 40, 6, 1)
        for p in range(NATM):
            ts[i, p, 0:HI, :] = total[p * HI : (p + 1) * HI, :]

    def scatter_forward(i):
        got = rcv.at[i, 0].reshape(NT, 128)[...]
        vf[0 : NT // 2, :] = jnp.where(first_half(NT // 2), got[0 : NT // 2], pltpu.roll(got[NT // 2 : NT], CAP, 1))
        vf[NT // 2 :, :] = rcv.at[i, 1].reshape(NT, 128)[...]
        total = scatter(vf, frow, hot_f, 3 * BLOCKS // 2, 24, 9, 0)
        for r in range(6):
            first = (8, 11, 0, 3, 16, 19)[r]
            for c in range(3):
                ls = slice(c * 128, (c + 1) * 128)
                f[i, r, 0:1, ls] = f[i, r, 0:1, ls] + total[first + c : first + c + 1, :] * st[r, 1:2, ls]

    def term_sum(slots):
        total = slots[0] + slots[1]
        for p in range(2, NATM):
            total = total + jnp.where(ocean, slots[p], 0.0)
        return total

    def put_hot(index, hot, start, stop):
        cell = lax.broadcasted_iota(I32, (128, 128), 0)

        @pl.loop(start, stop)
        def _(i):
            rows = index[pl.ds(pl.multiple_of(i * 8, 8), 8), :]
            for j in range(8):
                hit = jnp.where(cell == rows[j : j + 1, :], 1.0, 0.0).astype(BF16)
                hot[i, :, j * 128 : (j + 1) * 128] = hit

    def put_hot_columns(cells, first, start, count):
        target = lax.broadcasted_iota(I32, (128, 128), 1)

        @pl.loop(0, count)
        def _(i):
            columns = pltpu.roll(cells[...], lax.rem(128 - 8 * (first + i), 128), 1)
            for j in range(8):
                hit = jnp.where(target == columns[:, j : j + 1], 1.0, 0.0).astype(BF16)
                hot_f[start + i, j * 128 : (j + 1) * 128, :] = hit

    for n in LOAD_ORDER[:6]:
        loads[n].wait()
    diag = lax.broadcasted_iota(I32, (LEV, LEV), 0) == lax.broadcasted_iota(I32, (LEV, LEV), 1)
    for m in range(LEV):
        row = mix_ref[m]
        mat[m : m + 1, :] = row
        mtb[m] = jnp.broadcast_to(jnp.sum(jnp.where(diag, row, 0.0), axis=1, keepdims=True), (LEV, 128))
    for n in range(LEV):
        mb[n] = jnp.broadcast_to(mat[:, n : n + 1], (LEV, 128))
    for r in (0, 1):
        f[0, 2 + r] = init_ref[:, r, :]
        sp[2 + r] = spread_ref[:, r, :]
        te[0, 2 + r] = traj_ref[0, :, r, :]
        te[1, 2 + r] = traj_ref[2, :, r, :]
        to[0, 2 + r] = traj_ref[1, :, r, :]
        to[1, 2 + r] = traj_ref[3, :, r, :]
        xa[2 + r] = to[1, 2 + r] * cot_ref[:, r, :]
        st[2 + r, 0:1, :] = traj_ref[1, 0, r : r + 1, :]
        st[2 + r, 1:2, :] = sea_ref[r : r + 1, :].astype(F32)
    for r in (2, 3):
        u[0, r] = mix_row(xa, r, mtb)
    put_surface(0)
    for r in (2, 3):
        wa[r] = sp[r] * u[0, r]
    for side, near in ((0, 2), (1, 3)):
        far = 5 - near
        product = wa[near]
        reach = SPREAD * te[1, near] * sp[near]
        share = te[1, near] * u[0, near] + reach * (wa[far] + sideways(product) - 4.0 * product)
        pack(edge_s.at[side], [product, reach, level_zero(share), sp[near, 0:1, :]])
        pack(rest_s.at[side], [share, sp[near]])
        pack(first_s.at[side], [f[0, 2], f[0, 3], te[0, near], sp[far], st[2], st[3]])

    edge = jnp.where((z == 0) | (z == NZ - 1), 1, 0)
    pl.semaphore_wait(barrier, NY - 1 + len(NEAR_Z) + edge + jnp.where(atmos, 3 * (NG - NATM), 3 * NATM))
    beside_send(EDGE, edge_s.at[0], edge_s.at[1], edge_r)
    for d in column:
        pl.semaphore_signal(known, inc=1, device_id=(g, d), device_id_type=MESH)
    surface_send(0)

    for n in LOAD_ORDER[6:]:
        loads[n].wait()
    for h in range(HI):
        seat[h : h + 1, :] = st[2 + h // 3, 1:2, (h % 3) * 128 : (h % 3 + 1) * 128]
    live = lax.broadcasted_iota(I32, (CAP, NT), 0) < cnt_ref[...]
    weight = jnp.where(live, w_ref[...], 0.0)
    wv[...] = jnp.concatenate([weight, weight], axis=0).T
    aw[...] = packed(wv[...])
    srcc, dstc = srcc_ref[...], dst_ref[...]
    srcg = srcg_ref[...] - jnp.where(atmos, NATM, 0)
    gi[...] = jnp.concatenate([srcg, srcg], axis=0).T
    send_cell = jnp.concatenate([srcc, srcc], axis=0).T
    slo[...] = jnp.bitwise_and(send_cell, 127)
    shi[...] = jnp.right_shift(send_cell, 7)
    alo[...] = packed(slo[...])
    arow[...] = HI * packed(gi[...]) + packed(shi[...])
    come = packed(jnp.concatenate([dstc, dstc], axis=0).T)
    plo[...] = jnp.bitwise_and(come, 127)
    phi[...] = jnp.right_shift(come, 7)
    frow[0 : NT // 2, :] = phi[...]
    val[0:8, :] = jnp.zeros((8, 128), F32)
    val[8 + NT : 16 + NT, :] = jnp.zeros((8, 128), F32)

    put_hot(alo, hot_a, 0, BLOCKS // 2)
    cells[0:CAP, 0 : NT // 2] = jnp.bitwise_and(dstc[:, 0 : NT // 2], 127)
    cells[CAP:, 0 : NT // 2] = jnp.bitwise_and(dstc[:, NT // 2 :], 127)
    put_hot_columns(cells, 0, 0, BLOCKS // 2)
    beside_send(REST, rest_s.at[0], rest_s.at[1], rest_r)
    beside_send(DN, dst_ref, dst_ref, dn)

    pl.semaphore_wait(known, NY - 1)
    for b in (2, NZ - 2):
        pl.semaphore_signal(known_row, inc=1, device_id=(g, ys[0] + zs[b]), device_id_type=MESH)
    partner_wait(rsem, S0, ev.at[0])
    gather_forward(ev.at[0])
    put_beside(0)
    wait_bytes(rsem, EDGE, edge_r)
    beyond = ((0, 1, 0, t > 0), (1, 4, 5, t < NT - 1))
    for side, near, far, inside in beyond:
        wa[near] = jnp.where(inside, edge_r[side, 0:LEV, :], 0.0)
    first_surface()

    def unpack_pair(buf, i, landing):
        for side, rows in ((0, (0, 1)), (1, (4, 5))):
            for k, r in enumerate(rows):
                buf[i, r] = landing[side, k * LEV : (k + 1) * LEV, :]

    @pl.loop(0, 2)
    def _(i):
        @pl.when(i == 1)
        def _():
            adjoint_pair(1)

        put_masked()
        gather_adjoint()
        @pl.when(i == 1)
        def _():
            partner_wait(rsem, S0 + 1, ev.at[1])
            gather_forward(ev.at[1])
            put_beside(1)

        @pl.when(i == 0)
        def _():
            pl.semaphore_wait(known_row, 2)

        send_slots(i)

        @pl.when(i == 0)
        def _():
            beside_send(FIRST, first_s.at[0], first_s.at[1], first_r)
            wait_bytes(rsem, DN, dn)
            nearby = jnp.concatenate([dn[0], dn[1]], axis=0)
            cells[:, 0:NT] = jnp.bitwise_and(nearby, 127)
            frow[NT // 2 :, :] = jnp.right_shift(nearby.T, 7) + jnp.where(first_half(NT), 8, 16)
            put_hot_columns(cells, 0, BLOCKS // 2, BLOCKS // 2)
            wait_bytes(rsem, REST, rest_r)
            for side, near, far, inside in beyond:
                xa[near] = xa[near] + rest_r[side, 0:LEV, :]
                sp[near] = jnp.where(inside, rest_r[side, LEV : 2 * LEV, :], 0.0)
            second_step()
            for r in (2, 3):
                xa[r] = to[0, r] * adj[r]
            for r in (2, 3):
                u[1, r] = mix_row(xa, r, mtb)
            for side, near in ((0, 2), (1, 3)):
                pack(back_s.at[side], [u[1, 2], u[1, 3], te[1, near]])
            beside_send(BACK, back_s.at[0], back_s.at[1], back_r)
            put_hot_columns(cells, BLOCKS // 2, BLOCKS, BLOCKS // 2)

        @pl.when(i == 1)
        def _():
            beside_send(NEXT, next_s, next_s, next_r)
            for k, ref in ((REST, rest_s), (EDGE, edge_s), (FIRST, first_s), (BACK, back_s), (DN, dn)):
                wait_bytes(ssem, k, ref)
            partner_wait(ssem, S0, ev.at[0])
            partner_wait(ssem, S0 + 1, ev.at[1])
            partner_wait(ssem, TO, tro.at[0])
            sides_wait(ssem)
            wait_bytes(ssem, A0, rcv.at[0, :, 0 : NT - 1])

        wait_bytes(rsem, A0 + i, rcv.at[i, :, 0 : NT - 1])
        scatter_adjoint(i)
        @pl.when(i == 0)
        def _():
            each_partner(
                lambda p, d: [
                    remote(TS, ts.at[0, p], trs.at[1, me], (d, left)).start(),
                    remote(TS, ts.at[0, p], trs.at[0, me], (d, right)).start(),
                ]
            )

        each_partner(lambda p, d: remote(TO + i, ts.at[i, p], tro.at[i, me], (d, t)).start())
        @pl.when(i == 0)
        def _():
            wait_bytes(rsem, FIRST, first_r)
            unpack_pair(f, 0, first_r)
            for side, near, far, inside in beyond:
                got = first_r.at[side]
                te[0, near] = got[2 * LEV : 3 * LEV, :]
                sp[far] = jnp.where(inside, got[3 * LEV : 4 * LEV, :], 0.0)
                for k in range(2):
                    st[4 * side + k] = got[4 * LEV + 2 * k : 4 * LEV + 2 * k + 2, :]

        @pl.when(i == 1)
        def _():
            wait_bytes(rsem, NEXT, next_r)
            unpack_pair(f, 1, next_r)

        scatter_forward(i)
        forward_pair(i)

        @pl.when(i == 0)
        def _():
            put_surface(1)
            surface_send(1)
            pack(next_s, [f[1, 2], f[1, 3]])
            wait_bytes(rsem, BACK, back_r)
            unpack_pair(u, 1, back_r)
            for side, near, far, inside in beyond:
                te[1, near] = back_r[side, 2 * LEV : 3 * LEV, :]
            partner_wait(rsem, TO, tro.at[0])
            sides_wait(rsem)
            for k, slots in enumerate((trs.at[0], tro.at[0], trs.at[1])):
                part = term_sum(slots)
                for e in range(2):
                    r = 2 * k + e
                    for c in range(3):
                        ls = slice(c * 128, (c + 1) * 128)
                        q = part[3 * e + c : 3 * e + c + 1, :] * st[r, 0:1, ls]
                        u[1, r, :, ls] = u[1, r, :, ls] + mtb[0] * q

    for r in (2, 3):
        out_ref[0, :, r - 2, :] = f[2, r]
        out_ref[1, :, r - 2, :] = adj[r]
    wait_bytes(ssem, NEXT, next_r)
    wait_bytes(ssem, A0 + 1, rcv.at[1, :, 0 : NT - 1])
    partner_wait(rsem, TO + 1, tro.at[1])
    part = term_sum(tro.at[1])
    for h in range(HI):
        ls = slice((h % 3) * 128, (h % 3 + 1) * 128)
        out_ref[1, 0, h // 3 : h // 3 + 1, ls] = adj[2 + h // 3, 0:1, ls] + part[h : h + 1, :]
    partner_wait(ssem, TO + 1, tro.at[1])


def per_device(
    initial, cotangent, spread_coef, trajectory, mixing, sea_mask, src_group, src_cell, weight, counts, dst_cell
):
    vmem = lambda *shape, dtype=F32: pltpu.VMEM(shape, dtype)
    field = vmem(6, LEV, COLS)
    operands = (
        initial[0], cotangent[0], spread_coef[0], trajectory[:, 0], jnp.transpose(mixing, (1, 0, 2)), sea_mask[0],
        src_group[0, 0].T, src_cell[0, 0].T, weight[0, 0].T, counts[0], dst_cell[0, 0].T,
    )
    (both,) = pl.pallas_call(
        kernel,
        out_shape=[jax.ShapeDtypeStruct((2, LEV, 2, COLS), F32)],
        in_specs=[pl.BlockSpec(memory_space=pltpu.HBM)] * 11,
        out_specs=[pl.BlockSpec(memory_space=pltpu.VMEM)],
        scratch_shapes=[pltpu.VMEM(a.shape, a.dtype) for a in operands]
        + [vmem(3, 6, LEV, COLS), vmem(2, 6, LEV, COLS), vmem(2, 6, LEV, COLS), vmem(2, 6, LEV, COLS)]
        + [field] * 6
        + [vmem(6, 2, COLS)]
        + [vmem(2, 2 * LEV + 2, COLS)] * 2
        + [vmem(2, 2 * LEV, COLS)] * 2
        + [vmem(2, 56, COLS)] * 2
        + [vmem(2, 40, COLS)] * 2
        + [vmem(24, COLS), vmem(2, 24, COLS)]
        + [vmem(2, CAP, NT, dtype=I32)]
        + [vmem(2, NATM + 1, 8, 128)]
        + [vmem(2, NATM, 8, 128)] * 3
        + [vmem(2, 2, NT, 1, 128)] * 2
        + [vmem(LEV, LEV)]
        + [vmem(LEV, LEV, 128)] * 2
        + [vmem(8, 128)] * 2
        + [vmem(NT, 128, dtype=I32)] * 3
        + [vmem(NT, 128), vmem(NT + 16, 128)]
        + [vmem(NT // 2, 128, dtype=I32)] * 2
        + [vmem(NT // 2, 128)]
        + [vmem(NT // 2, 128, dtype=I32)] * 2
        + [vmem(NT // 2, 128)] * 2
        + [vmem(128, 128, dtype=I32), vmem(3 * NT // 2, 128, dtype=I32)]
        + [vmem(3 * NT // 2, 128)]
        + [vmem(BLOCKS // 2, 128, 1024, dtype=BF16), vmem(3 * BLOCKS // 2, 1024, 128, dtype=BF16)]
        + [pltpu.SemaphoreType.DMA((13,))] * 2
        + [pltpu.SemaphoreType.DMA((11,)), pltpu.SemaphoreType.REGULAR, pltpu.SemaphoreType.REGULAR],
        compiler_params=pltpu.CompilerParams(
            collective_id=0, has_side_effects=True, vmem_limit_bytes=40 * 1024 * 1024
        ),
    )(*[pltpu.with_memory_space_constraint(a, pltpu.HBM) for a in operands])
    return both[0:1], both[1:2]


def solution(mesh):
    return jax.shard_map(
        per_device,
        mesh=mesh,
        in_specs=(
            P("comp", None, "tile", None),
            P("comp", None, "tile", None),
            P("comp", None, "tile", None),
            P(None, "comp", None, "tile", None),
            P("comp", None, None),
            P("comp", "tile", None),
            P("comp", "tile", None, None),
            P("comp", "tile", None, None),
            P("comp", "tile", None, None),
            P("comp", "tile", None),
            P("comp", "tile", None, None),
        ),
        out_specs=(P("comp", None, "tile", None), P("comp", None, "tile", None)),
        check_vma=False,
    )
```
